32 devices in a mesh: dp: 8 (over y, x, core), seq: 4 (over z).
Axes of the slice: x: 2, y: 2, z: 4, core: 2. Of those that a mesh axis runs over, the one named last changes fastest.
Arguments:
- inputs: bfloat16 [8, 2048, 1472], P('dp', 'seq'), may hold values from -6 to 6
- segments: int32 [8, 2048], P('dp', 'seq'), may hold values from 0 to 5, never falling along the last dimension, each value on 1 to 800 neighbouring positions
- cotangent: bfloat16 [8, 2048, 1472], P('dp', 'seq'), may hold values from -6 to 6
- w_query: bfloat16 [1472, 384], P('dp', 'seq'), may hold values from -0.0546875 to 0.0546875
- w_key: bfloat16 [1472, 384], P('dp', 'seq'), may hold values from -0.109375 to 0.109375
- w_value: bfloat16 [1472, 384], P('dp', 'seq'), may hold values from -0.15625 to 0.15625
- w_out: bfloat16 [384, 1472], P('seq', 'dp'), may hold values from -1.25 to 1.25
- w_gate: bfloat16 [1472, 3584], P('dp', 'seq'), may hold values from -0.15625 to 0.15625
- w_up: bfloat16 [1472, 3584], P('dp', 'seq'), may hold values from -0.15625 to 0.15625
- w_down: bfloat16 [3584, 1472], P('seq', 'dp'), may hold values from -0.1875 to 0.1875
- gain_attn: bfloat16 [1472], P('dp'), may hold values from 0.25 to 1.75
- gain_ffn: bfloat16 [1472], P('dp'), may hold values from 0.25 to 1.75
- rel_table: bfloat16 [32, 6], P('dp'), may hold values from -4 to 4
Outputs:
- outputs: bfloat16 [8, 2048, 1472], P('dp', 'seq')
- input_grad: bfloat16 [8, 2048, 1472], P('dp', 'seq')
- grad_query: float32 [1472, 384], P('dp', 'seq')
- grad_key: float32 [1472, 384], P('dp', 'seq')
- grad_value: float32 [1472, 384], P('dp', 'seq')
- grad_out: float32 [384, 1472], P('seq', 'dp')
- grad_gate: float32 [1472, 3584], P('dp', 'seq')
- grad_up: float32 [1472, 3584], P('dp', 'seq')
- grad_down: float32 [3584, 1472], P('seq', 'dp')
- grad_gain_attn: float32 [1472], P('dp')
- grad_gain_ffn: float32 [1472], P('dp')
- grad_table: float32 [32, 6], P('dp')
The draws below stay inside these ranges and needn't reach their ends.
Inputs may be any that keep to these rules, and one draw needn't show every extreme that they name: `segments`: along each sequence the ids never fall; each id names one document of 1 to 800 tokens.
All inputs are finite; a program needn't handle non-finite values.
Results may differ from the reference program's by a relative error of at most 0.02.
Values may be sent and summed in bfloat16 or wider, within the bound.
No kernel may reach another device: no remote copies, remote signals or barrier semaphores. Data moves between devices by JAX's collectives and lax.ppermute only.
A program may use at most 256 MiB of HBM per device.

```python
import math
from functools import partial
import jax
import jax.numpy as jnp
import numpy as np
from jax import lax

D = 1472
HEADS = 6
INNER = 384
FF = 3584
BUCKETS = 32
LENGTH = 2048
SEQS = 8


def steps_of(own_key, extent, shards, smallest, top_value):
    def one(axis_at, blocks):
        draws = jax.random.uniform(jax.random.fold_in(jax.random.fold_in(own_key, 6), axis_at), (blocks,), jnp.float32, smallest / len(shards), top_value / len(shards))
        return jnp.repeat(jnp.exp(draws), extent[axis_at] // blocks).reshape((-1,) + (1,) * (len(extent) - axis_at - 1))

    level = one(*shards[0])
    for cut in shards[1:]:
        level = level * one(*cut)
    return level


def length_profile(count, total, limit, lean):
    portions = [(1 << 20) // math.isqrt(rank ** lean) + 1 for rank in range(2, count + 1)]
    spare, given = total - limit - (count - 1), [1] * (count - 1)
    while spare > 0:
        free = [i for i in range(count - 1) if given[i] < limit]
        whole, remaining = sum([portions[i] for i in free]), spare
        for i in free:
            more = min(limit - given[i], max(1, remaining * portions[i] // whole), spare)
            given[i] = given[i] + more
            spare = spare - more
    return np.array([limit] + given)


def uneven(own_key, amount, total, reach, slope):
    if amount == 2:
        one = jax.random.randint(own_key, (), max(1, total - reach), min(reach, total - 1) + 1)
        return jnp.stack([one, total - one])
    lengths = jnp.asarray(length_profile(amount, total, reach, slope), jnp.int32)
    couples = (amount - 1) // 2
    source_of, taker = lengths[1:1 + 2 * couples:2], lengths[2:2 + 2 * couples:2]
    slack = jnp.minimum(source_of - 1, reach - taker)
    moved = jax.random.randint(jax.random.fold_in(own_key, 1), (couples,), 0, 1 << 20) % (slack + 1)
    lengths = lengths.at[1:1 + 2 * couples:2].set(source_of - moved).at[2:2 + 2 * couples:2].set(taker + moved)
    return lengths[jax.random.permutation(jax.random.fold_in(own_key, 2), amount)]


def normal_values(own_key, shape, spread, limit, shards=(), kind=jnp.bfloat16):
    values = jax.random.normal(own_key, shape, jnp.float32) * spread
    if len(shards) > 0:
        values = steps_of(own_key, shape, shards, -0.22, 0.18) * values
    return jnp.clip(values, min=-limit, max=limit).astype(kind)


def setup_inputs(seed: int = 0) -> dict:
    seeds = jax.random.split(jax.random.key(seed), 14)
    inputs = normal_values(seeds[0], (SEQS, LENGTH, D), 1.0, 6.0, ((0, 8), (1, 4)))
    segments = jax.vmap(lambda own: jnp.searchsorted(jnp.cumsum(uneven(own, 6, LENGTH, LENGTH * 25 // 64, 0)), jnp.arange(LENGTH), side="right"))(jax.random.split(seeds[1], SEQS)).reshape((SEQS, LENGTH)).astype(jnp.int32)
    cotangent = normal_values(seeds[2], (SEQS, LENGTH, D), 1.0, 6.0, ((0, 8), (1, 4)))
    w_query = normal_values(seeds[3], (D, INNER), (D * 8) ** -0.5, 0.0546875, ((0, 8), (1, 4)))
    w_key = normal_values(seeds[4], (D, INNER), (D * 2) ** -0.5, 0.109375, ((0, 8), (1, 4)))
    w_value = normal_values(seeds[5], (D, INNER), D ** -0.5, 0.15625, ((0, 8), (1, 4)))
    w_out = normal_values(seeds[6], (INNER, D), (INNER // 16) ** -0.5, 1.25, ((0, 4), (1, 8)))
    w_gate = normal_values(seeds[7], (D, FF), D ** -0.5, 0.15625, ((0, 8), (1, 4)))
    w_up = normal_values(seeds[8], (D, FF), D ** -0.5, 0.15625, ((0, 8), (1, 4)))
    w_down = normal_values(seeds[9], (FF, D), (FF // 4) ** -0.5, 0.1875, ((0, 4), (1, 8)))
    gain_attn = jnp.clip(1.0 + 0.15 * jax.random.normal(seeds[10], (D,), jnp.float32), 0.25, 1.75).astype(jnp.bfloat16)
    gain_ffn = jnp.clip(1.0 + 0.15 * jax.random.normal(seeds[11], (D,), jnp.float32), 0.25, 1.75).astype(jnp.bfloat16)
    rel_table = normal_values(seeds[12], (BUCKETS, HEADS), 1.0, 4.0, ((0, 8),))
    return dict(inputs=inputs, segments=segments, cotangent=cotangent, w_query=w_query, w_key=w_key, w_value=w_value, w_out=w_out, w_gate=w_gate, w_up=w_up, w_down=w_down, gain_attn=gain_attn, gain_ffn=gain_ffn, rel_table=rel_table)


@jax.custom_vjp
def low(v):
    return lax.optimization_barrier(v.astype(jnp.bfloat16)).astype(jnp.float32)

@jax.custom_vjp
def low_back(v):
    return v

def low_keep(v):
    return (low(v), None)

def low_pass(kept, grad):
    return (grad,)

def back_keep(v):
    return (v, None)

def back_low(kept, grad):
    return (low(grad),)
low.defvjp(low_keep, low_pass)
low_back.defvjp(back_keep, back_low)
epsilon = 1e-06
far_steps = np.array([12, 16, 23, 32, 46, 64, 91], np.int32)
highest = lax.Precision.HIGHEST

def bucket_of(relative):
    distance = jnp.abs(relative)
    levels = lax.optimization_barrier(jnp.sum((distance[..., None] >= jnp.asarray(far_steps)).astype(jnp.int32), axis=-1, dtype=jnp.int32))
    inside = jnp.where(distance < 8, distance, 8 + levels)
    return inside + 16 * (relative > 0).astype(jnp.int32)

def rms_norm(tensor, scaling):
    return tensor * lax.rsqrt(lax.optimization_barrier(jnp.mean(tensor * tensor, axis=-1, keepdims=True)) + epsilon) * scaling

def attend_block(keys_four, values_four, key_segs, lookup, block_item):
    query_block, query_segs, first_row = block_item
    span_rows = query_block.shape[1]
    positions = first_row + jnp.arange(span_rows, dtype=jnp.int32)
    relative = jnp.arange(LENGTH, dtype=jnp.int32)[None, :] - positions[:, None]
    bias_part = jnp.take(lookup, bucket_of(relative), axis=0)
    scores = low_back(jnp.einsum('gqhe,gkhe->ghqk', query_block, keys_four, precision=highest))
    scores = scores + jnp.transpose(bias_part, (2, 0, 1))[None]
    same_doc = query_segs[:, None, :, None] == key_segs[:, None, None, :]
    scores = jnp.where(same_doc, scores, -1e+30)
    probs = jax.nn.softmax(scores, axis=-1)
    return jnp.einsum('ghqk,gkhe->gqhe', low(probs), values_four, precision=highest)

def layer(group_segs, inputs, w_query, w_key, w_value, w_out, w_gate, w_up, w_down, gain_attn, gain_ffn, rel_table):
    groups = inputs.shape[0]
    block_rows = min(512, LENGTH)
    block_count = LENGTH // block_rows
    head_size = w_query.shape[1] // HEADS
    normed = low(rms_norm(inputs, gain_attn))
    query_rows = low_back(low(jnp.einsum('gld,di->gli', normed, w_query, precision=highest)))
    key_rows = low_back(low(jnp.einsum('gld,di->gli', normed, w_key, precision=highest)))
    value_rows = low_back(low(jnp.einsum('gld,di->gli', normed, w_value, precision=highest)))
    query_blocks = jnp.moveaxis(query_rows.reshape(groups, block_count, block_rows, HEADS, head_size), 1, 0)
    seg_blocks = jnp.moveaxis(group_segs.reshape(groups, block_count, block_rows), 1, 0)
    firsts = block_rows * jnp.arange(block_count, dtype=jnp.int32)
    keys_four = key_rows.reshape(groups, LENGTH, HEADS, head_size)
    values_four = value_rows.reshape(groups, LENGTH, HEADS, head_size)
    attended = lax.map(jax.checkpoint(partial(attend_block, keys_four, values_four, group_segs, rel_table)), (query_blocks, seg_blocks, firsts))
    attended = jnp.moveaxis(attended, 0, 1).reshape(groups, LENGTH, HEADS * head_size)
    attended = low_back(low(attended))
    mixed = inputs + low_back(jnp.einsum('gli,id->gld', attended, w_out, precision=highest))
    normed_two = low(rms_norm(mixed, gain_ffn))
    gate_rows = low_back(jnp.einsum('gld,df->glf', normed_two, w_gate, precision=highest))
    up_rows = low_back(jnp.einsum('gld,df->glf', normed_two, w_up, precision=highest))
    hidden = low(jax.nn.gelu(gate_rows, approximate=True) * up_rows)
    return mixed + jnp.einsum('glf,fd->gld', hidden, w_down, precision=highest)

def reference(inputs, segments, cotangent, w_query, w_key, w_value, w_out, w_gate, w_up, w_down, gain_attn, gain_ffn, rel_table):
    params = tuple((weight.astype(jnp.float32) for weight in (w_query, w_key, w_value, w_out, w_gate, w_up, w_down, gain_attn, gain_ffn, rel_table)))
    groups = inputs.shape[0] // 2
    shaped_in = inputs.reshape(groups, 2, LENGTH, D)
    shaped_seg = segments.reshape(groups, 2, LENGTH)
    shaped_cot = cotangent.reshape(groups, 2, LENGTH, D)

    def group_step(totals, group_item):
        batch_in, batch_seg, batch_cot = group_item
        result, pullback = jax.vjp(partial(layer, batch_seg), batch_in.astype(jnp.float32), *params)
        gradients = pullback(batch_cot.astype(jnp.float32))
        totals = tuple((earlier + latest for earlier, latest in zip(totals, gradients[1:])))
        return (totals, (result.astype(jnp.bfloat16), gradients[0].astype(jnp.bfloat16)))
    start_totals = tuple((jnp.zeros_like(weight) for weight in params))
    totals, (outs_all, grads_all) = lax.scan(group_step, start_totals, (shaped_in, shaped_seg, shaped_cot))
    return (outs_all.reshape(inputs.shape), grads_all.reshape(inputs.shape), totals[0], totals[1], totals[2], totals[3], totals[4], totals[5], totals[6], totals[7], totals[8], totals[9])
```

```python
import math
from functools import partial

import jax
import jax.numpy as jnp
import numpy as np
from jax import lax
from jax.experimental import pallas as pl
from jax.experimental.pallas import tpu as pltpu
from jax.sharding import PartitionSpec as P

HEADS = 6
BUCKETS = 32
MAX_DOC = 800
BLK = 256
SPAN = 1024
EPS = 1e-06
MASKED = -1e30
F32 = jnp.float32
BF16 = jnp.bfloat16
VMEM_CAP = 58 * 1024 * 1024
GELU_K = math.sqrt(2.0 / math.pi)
GELU_A = 0.044715


def bucket_table():
    relative = np.arange(SPAN) - SPAN // 2
    distance = np.abs(relative)
    steps = np.array([12, 16, 23, 32, 46, 64, 91])
    levels = (distance[:, None] >= steps[None, :]).sum(axis=1)
    inside = np.where(distance < 8, distance, 8 + levels)
    return (inside + 16 * (relative > 0)).astype(np.int32)


class Moves:
    def __init__(self, n_dp, n_seq):
        self.n_dp, self.n_seq = n_dp, n_seq
        plane = n_dp // 2
        side = int(round(math.sqrt(plane)))
        self.size = {"a": plane // side, "b": side, "c": 2, "z": n_seq}
        dp = lax.axis_index("dp")
        self.index = {
            "a": dp // (2 * side),
            "b": (dp // 2) % side,
            "c": dp % 2,
            "z": lax.axis_index("seq"),
        }

    def rotate(self, x, axis):
        n = self.size[axis]
        if axis == "z":
            return lax.ppermute(x, "seq", [(i, (i + 1) % n) for i in range(n)])
        pairs = []
        side = self.size["b"]
        for i in range(self.n_dp):
            a, b, c = i // (2 * side), (i // 2) % side, i % 2
            if axis == "a":
                a = (a + 1) % n
            elif axis == "b":
                b = (b + 1) % n
            else:
                c = 1 - c
            pairs.append((i, (a * side + b) * 2 + c))
        return lax.ppermute(x, "dp", pairs)

    def zperm(self, x, pairs):
        return lax.ppermute(x, "seq", pairs)

    def gather(self, x, axis, at=0):
        n, i = self.size[axis], self.index[axis]
        if n == 2:
            other = self.rotate(x, axis)
            return ordered(i == 0, x, other, at)
        parts = [x]
        for _ in range(n - 1):
            parts.append(self.rotate(parts[-1], axis))
        turned = jnp.stack(parts[::-1] + parts[::-1], 0)
        full = lax.dynamic_slice_in_dim(turned, n - 1 - i, n, 0)
        return jnp.moveaxis(full, 0, at)

    def scatter(self, x, axis, at=0, out=BF16):
        n, i = self.size[axis], self.index[axis]
        take = lambda k: lax.dynamic_index_in_dim(x, k, at, keepdims=False)
        if n == 2:
            other = self.rotate(take(1 - i), axis)
            return add(take(i), other, out)
        acc = take((i + n - 1) % n)
        for step in range(n - 1):
            got = self.rotate(acc, axis)
            last = step == n - 2
            acc = add(take((i + 2 * n - 2 - step) % n), got, out if last else BF16)
        return acc


def add(x, y, out):
    return (x.astype(F32) + y.astype(F32)).astype(out)


def ordered(first, x, y, at):
    return jnp.stack([jnp.where(first, x, y), jnp.where(first, y, x)], at)


def z_pairs(mv, w):
    z = mv.index["z"]
    near = mv.zperm(w, [(0, 1), (1, 0), (2, 3), (3, 2)])
    pair = ordered(z % 2 == 0, w, near, 0)
    mid = mv.zperm(pair, [(1, 2), (2, 1)])
    far = mv.zperm(mid, [(1, 0), (2, 3)])
    got = jnp.where((z == 1) | (z == 2), mid, far)
    return pair, got


def z_gather(mv, w):
    if mv.n_seq != 4:
        return mv.gather(w, "z")
    pair, got = z_pairs(mv, w)
    low = mv.index["z"] < 2
    return ordered(low, pair, got, 0).reshape((4,) + w.shape)


def core_halves(mv, w):
    c = mv.index["c"]
    if mv.n_seq == 4:
        pair, got = z_pairs(mv, w)
        mine = (mv.index["z"] // 2) == c
        return jnp.where(mine, pair, got), jnp.where(mine, got, pair)
    full = mv.gather(w, "z")
    halves = full.reshape((2, mv.n_seq // 2) + w.shape)
    take = lambda k: lax.dynamic_index_in_dim(halves, k, 0, keepdims=False)
    return take(c), take(1 - c)


def gather_ffn(mv, w):
    c = mv.index["c"]
    k, rows, cols = w.shape
    keep, send = core_halves(mv, w)
    recv = mv.rotate(send, "c")
    block = ordered(c == 0, keep, recv, 2)
    zh = block.shape[0]
    result = []
    for j in range(zh):
        one = block[j].reshape(k, 2 * rows, cols)
        if j % 2 == 0:
            one = mv.gather(one, "b", 1)
            one = mv.gather(one, "a", 1)
        else:
            one = mv.gather(one, "a", 1)
            one = mv.gather(one, "b", 2)
        result.append(one.reshape(k, mv.n_dp * rows, cols))
    return result


def scatter_ffn_plane(mv, grad, j):
    k, depth, cols = grad.shape
    rows = depth // mv.n_dp
    na, nb = mv.size["a"], mv.size["b"]
    x = grad.reshape(k, na, nb, 2 * rows, cols)
    if j % 2 == 0:
        x = mv.scatter(x, "a", 1)
        x = mv.scatter(x, "b", 1)
    else:
        x = mv.scatter(x, "b", 2)
        x = mv.scatter(x, "a", 1)
    x = x.reshape(k, 2, rows, cols)
    c = mv.index["c"]
    take = lambda i: lax.dynamic_index_in_dim(x, i, 1, keepdims=False)
    keep = take(c)
    recv = mv.rotate(take(1 - c), "c")
    return ordered(c == 0, keep, recv, 0)


def scatter_ffn_z(mv, planes):
    z = mv.index["z"]
    if mv.n_seq != 4:
        full = jnp.stack(planes, 1)
        full = full.reshape((mv.n_seq,) + planes[0].shape[1:])
        return mv.scatter(full, "z", 0, F32)
    sums = []
    for j, x in enumerate(planes):
        take = lambda i: lax.dynamic_index_in_dim(x, i, 0, keepdims=False)
        high = z // 2
        recv = mv.zperm(take(1 - high), [(0, 2), (2, 0), (1, 3), (3, 1)])
        part = add(take(high), recv, BF16)
        recv = mv.zperm(part, [(1 - j, j), (3 - j, 2 + j)])
        sums.append(add(part, recv, F32))
    return jnp.where(z % 2 == 0, sums[0], sums[1])


def gather_small(mv, w):
    full = z_gather(mv, w)
    half = mv.n_seq // 2
    lo = mv.gather(mv.gather(full[:half], "b", 1), "a", 1)
    hi = mv.gather(mv.gather(full[half:], "a", 1), "b", 2)
    both = jnp.concatenate([lo, hi], 0)
    both = mv.gather(both, "c", 3)
    return both.reshape((mv.n_seq, mv.n_dp) + w.shape)


def scatter_small(mv, g):
    na, nb = mv.size["a"], mv.size["b"]
    zs, _, rp, cols = g.shape
    x = g.reshape(zs, na, nb, 2, rp, cols)
    x = mv.scatter(x, "c", 3)
    half = zs // 2
    lo = mv.scatter(mv.scatter(x[:half], "a", 1), "b", 1)
    hi = mv.scatter(mv.scatter(x[half:], "b", 2), "a", 1)
    x = jnp.concatenate([lo, hi], 0)
    if zs != 4:
        return mv.scatter(x, "z", 0, F32)
    z = mv.index["z"]
    x = x.reshape(2, 2, rp, cols)
    take = lambda i: lax.dynamic_index_in_dim(x, i, 0, keepdims=False)
    recv = mv.zperm(take(1 - z // 2), [(0, 2), (2, 0), (1, 3), (3, 1)])
    x = add(take(z // 2), recv, BF16)
    take = lambda i: lax.dynamic_index_in_dim(x, i, 0, keepdims=False)
    recv = mv.zperm(take(1 - z % 2), [(0, 1), (1, 0), (2, 3), (3, 2)])
    return add(take(z % 2), recv, F32)


def halo(mv, x, fill):
    rows = x.shape[0]
    n = mv.n_seq
    need = MAX_DOC
    left, right = [], []
    step = 1
    while need > 0 and step < n:
        take = min(rows, need)
        up = x if take == rows else x[rows - take :]
        down = x if take == rows else x[:take]
        left.insert(0, mv.zperm(up, [(i, i + step) for i in range(n - step)]))
        right.append(mv.zperm(down, [(i + step, i) for i in range(n - step)]))
        need -= take
        step += 1
    have = sum(part.shape[0] for part in left)
    pad = jnp.zeros((fill - have,) + x.shape[1:], x.dtype)
    return jnp.concatenate([pad] + left + [x] + right + [pad], 0)


def nt(x, y):
    return lax.dot_general(x, y, (((1,), (1,)), ((), ())), preferred_element_type=F32)


def nn(x, y):
    return lax.dot_general(x, y, (((1,), (0,)), ((), ())), preferred_element_type=F32)


def make_tiles(vec_ref, tiles):
    for h in range(HEADS):
        line = vec_ref[h : h + 1, :]
        wide = jnp.broadcast_to(line, (BLK, SPAN))
        rolled = pltpu.roll(wide, 0, 1, stride=1, stride_axis=0)
        tiles[h * 5] = jnp.broadcast_to(line[:, :1], (BLK, BLK))
        tiles[h * 5 + 4] = jnp.broadcast_to(line[:, SPAN - 1 :], (BLK, BLK))
        for d in (-1, 0, 1):
            at = SPAN // 2 + BLK * d
            tiles[h * 5 + 2 + d] = rolled[:, at : at + BLK]


def pair_masks(x):
    lane = lax.broadcasted_iota(jnp.int32, x.shape, 1)
    zero = jnp.zeros_like(x)
    return jnp.where(lane < 64, x, zero), jnp.where(lane < 64, zero, x)


def class_of(kb, own):
    return jnp.clip(kb - own, -2, 2) + 2


def forward_kernel(off, lohi, vec, q_ref, segq, kv, segk, out, exact, lse, tiles):
    i = pl.program_id(0)

    @pl.when(i == 0)
    def _():
        make_tiles(vec, tiles)

    own = off // BLK + i
    inner = HEADS * 64
    low, high = lohi[i, 0], lohi[i, 1]
    lane = lax.broadcasted_iota(jnp.int32, (BLK, 128), 1)
    seg_col = segq[...]
    for pair in range(HEADS // 2):
        cols = slice(pair * 128, pair * 128 + 128)
        vcols = slice(inner + pair * 128, inner + pair * 128 + 128)
        qs = pair_masks(q_ref[:, cols])

        def body(kb, state):
            rows = pl.ds(pl.multiple_of(kb * BLK, BLK), BLK)
            keys, values = kv[rows, cols], kv[rows, vcols]
            same = seg_col == segk[kb]
            kind = class_of(kb, own)
            new = []
            for e in range(2):
                peak, total, acc = state[e]
                s = nt(qs[e], keys) + tiles[(pair * 2 + e) * 5 + kind]
                s = jnp.where(same, s, MASKED)
                top = jnp.maximum(peak, jnp.max(s, axis=1, keepdims=True))
                fade = jnp.exp(peak - top)
                p = jnp.exp(s - top)
                total = total * fade + jnp.sum(p, axis=1, keepdims=True)
                acc = acc * fade + nn(p.astype(BF16), values)
                new.append((top, total, acc))
            return tuple(new)

        start = (
            jnp.full((BLK, 1), MASKED, F32),
            jnp.zeros((BLK, 1), F32),
            jnp.zeros((BLK, 128), F32),
        )
        state = lax.fori_loop(low, high, body, (start, start))
        done = []
        for e in range(2):
            peak, total, acc = state[e]
            done.append(acc / total)
            h = pair * 2 + e
            lse[:, h : h + 1] = peak + jnp.log(total)
        merged = jnp.where(lane < 64, done[0], done[1])
        out[:, cols] = merged.astype(BF16)
        exact[:, cols] = merged


def query_kernel(off, lohi, vec, q_ref, do_ref, stat, segq, kv, segk, dq, near, far, tiles, sums):
    i = pl.program_id(0)

    @pl.when(i == 0)
    def _():
        make_tiles(vec, tiles)
        sums[...] = jnp.zeros_like(sums)

    own = off // BLK + i
    inner = HEADS * 64
    low, high = lohi[i, 0], lohi[i, 1]
    lane = lax.broadcasted_iota(jnp.int32, (BLK, 128), 1)
    seg_col = segq[...]
    for pair in range(HEADS // 2):
        cols = slice(pair * 128, pair * 128 + 128)
        vcols = slice(inner + pair * 128, inner + pair * 128 + 128)
        qs = pair_masks(q_ref[:, cols])
        dos = pair_masks(do_ref[:, cols])

        def body(kb, state):
            rows = pl.ds(pl.multiple_of(kb * BLK, BLK), BLK)
            keys, values = kv[rows, cols], kv[rows, vcols]
            same = seg_col == segk[kb]
            kind = class_of(kb, own)
            new = []
            for e in range(2):
                h = pair * 2 + e
                s = nt(qs[e], keys) + tiles[h * 5 + kind]
                s = jnp.where(same, s, MASKED)
                p = jnp.exp(s - stat[:, h : h + 1])
                dp = nt(dos[e], values)
                ds = p * (dp - stat[:, 8 + h : 9 + h])
                at = h * 5 + kind
                sums[at] = sums[at] + ds
                new.append(state[e] + nn(ds.astype(BF16), keys))
            return tuple(new)

        start = jnp.zeros((BLK, 128), F32)
        state = lax.fori_loop(low, high, body, (start, start))
        dq[:, cols] = jnp.where(lane < 64, state[0], state[1]).astype(BF16)

    @pl.when(i == pl.num_programs(0) - 1)
    def _():
        for h in range(HEADS):
            zero = jnp.zeros((BLK, BLK), F32)
            x = jnp.concatenate([sums[h * 5 + 1], sums[h * 5 + 2], sums[h * 5 + 3], zero], axis=1)
            n = BLK // 2
            while n >= 8:
                x = x[:n] + pltpu.roll(x[n:], SPAN - n, 1)
                n //= 2
            row = lax.broadcasted_iota(jnp.int32, x.shape, 0)
            for n in (4, 2, 1):
                x = jnp.where((row & n) != 0, pltpu.roll(x, SPAN - n, 1), x)
            near[h] = x
            far[h, 0] = jnp.sum(sums[h * 5].reshape(BLK // 8, 8, BLK), axis=0)
            far[h, 1] = jnp.sum(sums[h * 5 + 4].reshape(BLK // 8, 8, BLK), axis=0)


def key_kernel(off, lohi, vec, kv_ref, segk, qd, stat, segq, dkv, tiles):
    i = pl.program_id(0)

    @pl.when(i == 0)
    def _():
        make_tiles(vec, tiles)

    own = off // BLK + i
    inner = HEADS * 64
    low, high = lohi[i, 0], lohi[i, 1]
    lane = lax.broadcasted_iota(jnp.int32, (BLK, 128), 1)
    seg_col = segk[...]
    for pair in range(HEADS // 2):
        cols = slice(pair * 128, pair * 128 + 128)
        vcols = slice(inner + pair * 128, inner + pair * 128 + 128)
        ks = pair_masks(kv_ref[:, cols])
        vs = pair_masks(kv_ref[:, vcols])

        def body(qb, state):
            rows = pl.ds(pl.multiple_of(qb * BLK, BLK), BLK)
            queries, answers = qd[rows, cols], qd[rows, vcols]
            same = seg_col == segq[qb]
            kind = class_of(qb, own)
            new = []
            for e in range(2):
                h = pair * 2 + e
                s = nt(ks[e], queries) + tiles[h * 5 + kind]
                s = jnp.where(same, s, MASKED)
                p = jnp.exp(s - stat[qb, h : h + 1, :])
                dp = nt(vs[e], answers)
                ds = p * (dp - stat[qb, 8 + h : 9 + h, :])
                dk, dv = state[e]
                dk = dk + nn(ds.astype(BF16), queries)
                dv = dv + nn(p.astype(BF16), answers)
                new.append((dk, dv))
            return tuple(new)

        start = jnp.zeros((BLK, 128), F32)
        state = lax.fori_loop(low, high, body, ((start, start), (start, start)))
        dkv[:, cols] = jnp.where(lane < 64, state[0][0], state[1][0]).astype(BF16)
        dkv[:, vcols] = jnp.where(lane < 64, state[0][1], state[1][1]).astype(BF16)


def whole_block(shape):
    return pl.BlockSpec(shape, lambda i: (0,) * len(shape))


def row_block(cols):
    return pl.BlockSpec((BLK, cols), lambda i: (i, 0))


SMEM_SPEC = pl.BlockSpec(memory_space=pltpu.SMEM)
ATTN_PARAMS = dict(
    compiler_params=pltpu.CompilerParams(
        dimension_semantics=("arbitrary",), vmem_limit_bytes=VMEM_CAP
    )
)
TILES = pltpu.VMEM((HEADS * 5, BLK, BLK), F32)


def attend(off, lohi, vec, q, seg_col, kv, seg_row):
    rows, inner = q.shape
    return pl.pallas_call(
        partial(forward_kernel, off),
        grid=(rows // BLK,),
        in_specs=[
            SMEM_SPEC,
            whole_block(vec.shape),
            row_block(inner),
            row_block(1),
            whole_block(kv.shape),
            whole_block(seg_row.shape),
        ],
        out_specs=[row_block(inner), row_block(inner), row_block(128)],
        out_shape=[
            jax.ShapeDtypeStruct((rows, inner), BF16),
            jax.ShapeDtypeStruct((rows, inner), F32),
            jax.ShapeDtypeStruct((rows, 128), F32),
        ],
        scratch_shapes=[TILES],
        cost_estimate=pl.CostEstimate(
            flops=rows * 1280 * inner * 4 * 4, bytes_accessed=8 * 2**20, transcendentals=0
        ),
        name="attend",
        **ATTN_PARAMS,
    )(lohi, vec, q, seg_col, kv, seg_row)


def attend_queries(off, lohi, vec, q, do, stat, seg_col, kv, seg_row):
    rows, inner = q.shape
    return pl.pallas_call(
        partial(query_kernel, off),
        grid=(rows // BLK,),
        in_specs=[
            SMEM_SPEC,
            whole_block(vec.shape),
            row_block(inner),
            row_block(inner),
            row_block(128),
            row_block(1),
            whole_block(kv.shape),
            whole_block(seg_row.shape),
        ],
        out_specs=[
            row_block(inner),
            whole_block((HEADS, 8, SPAN)),
            whole_block((HEADS, 2, 8, BLK)),
        ],
        out_shape=[
            jax.ShapeDtypeStruct((rows, inner), BF16),
            jax.ShapeDtypeStruct((HEADS, 8, SPAN), F32),
            jax.ShapeDtypeStruct((HEADS, 2, 8, BLK), F32),
        ],
        scratch_shapes=[TILES, TILES],
        cost_estimate=pl.CostEstimate(
            flops=rows * 1280 * inner * 6 * 4, bytes_accessed=8 * 2**20, transcendentals=0
        ),
        name="attend_queries",
        **ATTN_PARAMS,
    )(lohi, vec, q, do, stat, seg_col, kv, seg_row)


def attend_keys(off, lohi, vec, kv, seg_col, qd, stat, seg_row):
    rows, wide = kv.shape
    return pl.pallas_call(
        partial(key_kernel, off),
        grid=(rows // BLK,),
        in_specs=[
            SMEM_SPEC,
            whole_block(vec.shape),
            row_block(wide),
            row_block(1),
            whole_block(qd.shape),
            whole_block(stat.shape),
            whole_block(seg_row.shape),
        ],
        out_specs=row_block(wide),
        out_shape=jax.ShapeDtypeStruct((rows, wide), BF16),
        scratch_shapes=[TILES],
        cost_estimate=pl.CostEstimate(
            flops=rows * 1280 * wide * 4 * 4, bytes_accessed=8 * 2**20, transcendentals=0
        ),
        name="attend_keys",
        **ATTN_PARAMS,
    )(lohi, vec, kv, seg_col, qd, stat, seg_row)


def ffn_kernel(nm, n2, ct, n2t, ctt, wg, wu, wd, out, gn2, dw, hid, ggr, gur):
    i = pl.program_id(0)

    @pl.when(i < nm)
    def _():
        rows = pl.ds(pl.multiple_of(i * BLK, BLK), BLK)
        x = n2[...]
        g = nn(x, wg[...])
        u = nn(x, wu[...])
        gh = nn(ct[...], wd[...])
        square = g * g
        t = jnp.tanh(GELU_K * g * (1.0 + GELU_A * square))
        half = 0.5 * (1.0 + t)
        gelu = g * half
        slope = half + 0.5 * g * (1.0 - t * t) * (GELU_K * (1.0 + 3.0 * GELU_A * square))
        h = (gelu * u).astype(BF16)
        gg = (gh * u * slope).astype(BF16)
        gu = (gh * gelu).astype(BF16)
        hid[rows, :] = h
        ggr[rows, :] = gg
        gur[rows, :] = gu
        out[...] = nt(h, wd[...]).astype(BF16)
        gn2[...] = (nt(gg, wg[...]) + nt(gu, wu[...])).astype(BF16)

    @pl.when(i >= nm)
    def _():
        x = n2t[...]
        dw[0] = nn(x, ggr[...]).astype(BF16)
        dw[1] = nn(x, gur[...]).astype(BF16)
        dw[2] = nn(ctt[...], hid[...]).astype(BF16)


def ffn(n2, ct, n2t, ctt, wg, wu, wd):
    m, depth = n2.shape
    cols = wg.shape[1]
    nm = m // BLK
    nr = 4
    tile = depth // nr
    first = lambda i: (jnp.minimum(i, nm - 1), 0)
    later = lambda i: (jnp.maximum(i - nm, 0), 0)
    weight = pl.BlockSpec((depth, cols), lambda i: (0, 0), pipeline_mode=pl.Buffered(1))
    return pl.pallas_call(
        partial(ffn_kernel, nm),
        grid=(nm + nr,),
        in_specs=[
            pl.BlockSpec((BLK, depth), first),
            pl.BlockSpec((BLK, depth), first),
            pl.BlockSpec((tile, m), later),
            pl.BlockSpec((tile, m), later),
            weight,
            weight,
            weight,
        ],
        out_specs=[
            pl.BlockSpec((BLK, depth), first),
            pl.BlockSpec((BLK, depth), first),
            pl.BlockSpec((3, tile, cols), lambda i: (0, jnp.maximum(i - nm, 0), 0)),
        ],
        out_shape=[
            jax.ShapeDtypeStruct((m, depth), BF16),
            jax.ShapeDtypeStruct((m, depth), BF16),
            jax.ShapeDtypeStruct((3, depth, cols), BF16),
        ],
        scratch_shapes=[pltpu.VMEM((m, cols), BF16)] * 3,
        cost_estimate=pl.CostEstimate(
            flops=18 * m * depth * cols, bytes_accessed=32 * 2**20, transcendentals=0
        ),
        name="ffn",
        compiler_params=pltpu.CompilerParams(
            dimension_semantics=("arbitrary",), vmem_limit_bytes=VMEM_CAP
        ),
    )(n2, ct, n2t, ctt, wg, wu, wd)


def rms_scale(x):
    return lax.rsqrt(jnp.mean(x * x, axis=-1, keepdims=True) + EPS)


def norm_back(grad, x, scale, gain):
    gain_grad = jnp.sum(grad * (x * scale), axis=0)
    weighted = grad * gain
    dots = jnp.mean(weighted * x, axis=-1, keepdims=True)
    return scale * weighted - x * (scale * scale * scale * dots), gain_grad


def split_heads_z(x, n_seq):
    rows, inner = x.shape
    return jnp.transpose(x.reshape(rows, n_seq, inner // n_seq), (1, 0, 2))


def on_device(
    n_dp,
    n_seq,
    inputs,
    segments,
    cotangent,
    w_query,
    w_key,
    w_value,
    w_out,
    w_gate,
    w_up,
    w_down,
    gain_attn,
    gain_ffn,
    rel_table,
):
    mv = Moves(n_dp, n_seq)
    seqs, rows, depth = inputs.shape
    source = inputs.reshape(seqs * rows, depth).astype(F32)
    tangent = cotangent.reshape(seqs * rows, depth)
    rw = w_query.shape[0]
    sc = w_query.shape[1]
    inner = sc * n_seq
    rp = -(-(rw + 2) // 16) * 16

    body = jnp.concatenate([w_query, w_key, w_value, w_out.T], axis=1)
    gains = jnp.concatenate([gain_attn, gain_ffn])
    table_row = rel_table.reshape(-1)
    pad_to = lambda v: jnp.pad(v, (0, 4 * sc - v.shape[0]))[None]
    packed = jnp.concatenate(
        [body, pad_to(gains), pad_to(table_row), jnp.zeros((rp - rw - 2, 4 * sc), BF16)], axis=0
    )
    att = gather_small(mv, packed)
    full = att[:, :, :rw, :].reshape(n_seq, depth, 4 * sc)
    gain_one = att[0, :, rw, :rw].reshape(depth).astype(F32)
    gain_two = att[0, :, rw, rw : 2 * rw].reshape(depth).astype(F32)
    table = att[0, :, rw + 1, : table_row.shape[0]].reshape(BUCKETS, HEADS)

    weights_down = gather_ffn(mv, w_down.T[None])
    weights_pair = gather_ffn(mv, jnp.stack([w_gate, w_up]))

    scale_one = rms_scale(source)
    normed = ((source * scale_one) * gain_one).astype(BF16)
    qkv = jnp.einsum("td,zdc->ztc", normed, full[:, :, : 3 * sc], preferred_element_type=F32)
    qkv = jnp.transpose(qkv.astype(BF16).reshape(n_seq, rows, 3, sc), (1, 2, 0, 3))
    qkv = qkv.reshape(rows, 3 * inner)
    q = qkv[:, :inner]
    kv = qkv[:, inner:]

    off = -(-MAX_DOC // BLK) * BLK
    blocks = (2 * off + rows) // BLK
    seg_own = segments.reshape(rows)
    seg_all = halo(mv, (seg_own + 1).reshape(rows, 1), off)[:, 0] - 1
    seg_row = seg_all.reshape(blocks, 1, BLK)
    seg_col = seg_own.reshape(rows, 1)
    spots = jnp.arange(seg_all.shape[0], dtype=jnp.int32)
    firsts = seg_own[::BLK]
    lasts = seg_own[BLK - 1 :: BLK]
    low = jnp.min(jnp.where(seg_all[None] == firsts[:, None], spots[None], 1 << 20), axis=1) // BLK
    high = jnp.max(jnp.where(seg_all[None] == lasts[:, None], spots[None], -1), axis=1) // BLK + 1
    lohi = jnp.stack([low, high], 1).astype(jnp.int32)

    buckets = bucket_table()
    chosen = jnp.asarray((buckets[:, None] == np.arange(BUCKETS)[None, :]), BF16)
    vec = lax.dot_general(
        table, chosen, (((0,), (1,)), ((), ())), preferred_element_type=F32
    )
    vec_back = jnp.roll(vec[:, ::-1], 1, axis=1)
    vec_back = vec_back.at[:, 0].set(vec[:, SPAN - 1])

    kv_all = halo(mv, kv, off)
    attended, exact, lse = attend(off, lohi, vec, q, seg_col, kv_all, seg_row)
    q_all = halo(mv, q, off)

    mixed = source + jnp.einsum(
        "tzc,zdc->td",
        attended.reshape(rows, n_seq, sc),
        full[:, :, 3 * sc :],
        preferred_element_type=F32,
    )
    scale_two = rms_scale(mixed)
    normed_two = ((mixed * scale_two) * gain_two).astype(BF16)

    n2 = jnp.concatenate([normed_two, mv.rotate(normed_two, "c")], 0)
    ct = jnp.concatenate([tangent, mv.rotate(tangent, "c")], 0)
    n2t, ctt = n2.T, ct.T
    outs, gn2s, planes = [], [], []
    for j in range(n_seq // 2):
        out_part, gn2_part, dw = ffn(
            n2, ct, n2t, ctt, weights_pair[j][0], weights_pair[j][1], weights_down[j][0]
        )
        outs.append(out_part.astype(F32))
        gn2s.append(gn2_part.astype(F32))
        planes.append(scatter_ffn_plane(mv, dw, j))
    gn2 = sum(gn2s)
    grad_n2 = gn2[:rows] + mv.rotate(gn2[rows:].astype(BF16), "c").astype(F32)
    out_sum = sum(outs)
    outputs = mixed + out_sum[:rows] + mv.rotate(out_sum[rows:].astype(BF16), "c").astype(F32)
    outputs = outputs.astype(BF16)
    own_ffn = scatter_ffn_z(mv, planes)

    grad_mixed, grad_gain_two = norm_back(grad_n2, mixed, scale_two, gain_two)
    grad_mixed = grad_mixed + tangent.astype(F32)
    grad_branch = grad_mixed.astype(BF16)
    grad_att = jnp.einsum(
        "td,zdc->tzc", grad_branch, full[:, :, 3 * sc :], preferred_element_type=F32
    )
    grad_att = grad_att.reshape(rows, inner).astype(BF16)
    delta = jnp.sum(
        (grad_att.astype(F32) * exact).reshape(rows, HEADS, inner // HEADS), axis=2
    )
    stat = jnp.concatenate([lse[:, :8], jnp.pad(delta, ((0, 0), (0, 120)))], axis=1)
    stat_all = halo(mv, stat[:, :16], off)
    stat_rows = jnp.transpose(stat_all.reshape(blocks, BLK, 16), (0, 2, 1))
    qd_all = jnp.concatenate([q_all, halo(mv, grad_att, off)], axis=1)

    dq, near, far = attend_queries(off, lohi, vec, q, grad_att, stat, seg_col, kv_all, seg_row)
    dkv = attend_keys(off, lohi, vec_back, kv, seg_col, qd_all, stat_rows, seg_row)

    sheared = jnp.sum(near, axis=1)
    sheared = jnp.roll(sheared, BLK, axis=1)
    grad_table = jnp.dot(
        sheared, chosen.astype(F32), precision=lax.Precision.HIGHEST
    ).T
    far_sums = jnp.sum(far, axis=(2, 3))
    grad_table = grad_table.at[15].add(far_sums[:, 0]).at[31].add(far_sums[:, 1])

    rows_z = jnp.concatenate(
        [split_heads_z(dq, n_seq), split_heads_z(dkv[:, :inner], n_seq), split_heads_z(dkv[:, inner:], n_seq)],
        axis=2,
    )
    grad_normed = jnp.einsum(
        "ztc,zdc->td", rows_z, full[:, :, : 3 * sc], preferred_element_type=F32
    )
    grad_source, grad_gain_one = norm_back(grad_normed, source, scale_one, gain_one)
    input_grad = (grad_mixed + grad_source).astype(BF16)

    g_in = jnp.einsum("td,ztc->zdc", normed, rows_z, preferred_element_type=F32)
    g_out = jnp.einsum(
        "td,ztc->zdc", grad_branch, split_heads_z(attended, n_seq), preferred_element_type=F32
    )
    grads = jnp.concatenate([g_in, g_out], axis=2).reshape(n_seq, n_dp, rw, 4 * sc)
    gain_rows = jnp.concatenate(
        [grad_gain_one.reshape(n_dp, rw), grad_gain_two.reshape(n_dp, rw)], axis=1
    )
    widen = lambda v: jnp.broadcast_to(
        jnp.pad(v, ((0, 0), (0, 4 * sc - v.shape[1])))[None, :, None, :], (n_seq, n_dp, 1, 4 * sc)
    )
    table_rows = grad_table.reshape(n_dp, -1)
    grads = jnp.concatenate(
        [
            grads,
            widen(gain_rows),
            widen(table_rows),
            jnp.zeros((n_seq, n_dp, rp - rw - 2, 4 * sc), F32),
        ],
        axis=2,
    ).astype(BF16)
    own = scatter_small(mv, grads)

    return (
        outputs.reshape(seqs, rows, depth),
        input_grad.reshape(seqs, rows, depth),
        own[:rw, :sc],
        own[:rw, sc : 2 * sc],
        own[:rw, 2 * sc : 3 * sc],
        own[:rw, 3 * sc :].T,
        own_ffn[0],
        own_ffn[1],
        own_ffn[2].T,
        own[rw, :rw],
        own[rw, rw : 2 * rw],
        own[rw + 1, : table_row.shape[0]].reshape(rel_table.shape),
    )


def solution(mesh):
    row, col = P("dp", "seq"), P("seq", "dp")
    tokens = P("dp", "seq", None)
    return jax.shard_map(
        partial(on_device, mesh.shape["dp"], mesh.shape["seq"]),
        mesh=mesh,
        in_specs=(tokens, row, tokens, row, row, row, col, row, row, col, P("dp"), P("dp"), P("dp", None)),
        out_specs=(tokens, tokens, row, row, row, col, row, row, col, P("dp"), P("dp"), P("dp", None)),
        check_vma=False,
    )
```

```python
import math
from functools import partial

import jax
import jax.numpy as jnp
import numpy as np
from jax import lax
from jax.experimental import pallas as pl
from jax.experimental.pallas import tpu as pltpu
from jax.sharding import PartitionSpec as P

HEADS = 6
BUCKETS = 32
MAX_DOC = 800
BLK = 256
SPAN = 1024
EPS = 1e-06
MASKED = -1e30
F32 = jnp.float32
BF16 = jnp.bfloat16
VMEM_CAP = 58 * 1024 * 1024
LANES = 128
GELU_K = math.sqrt(2.0 / math.pi)
GELU_A = 0.044715


def bucket_table():
    relative = np.arange(SPAN) - SPAN // 2
    distance = np.abs(relative)
    steps = np.array([12, 16, 23, 32, 46, 64, 91])
    levels = (distance[:, None] >= steps[None, :]).sum(axis=1)
    inside = np.where(distance < 8, distance, 8 + levels)
    return (inside + 16 * (relative > 0)).astype(np.int32)


class Moves:
    def __init__(self, n_dp, n_seq):
        self.n_dp, self.n_seq = n_dp, n_seq
        plane = n_dp // 2
        side = int(round(math.sqrt(plane)))
        self.size = {"a": plane // side, "b": side, "c": 2, "z": n_seq}
        dp = lax.axis_index("dp")
        self.last = {}
        self.index = {
            "a": dp // (2 * side),
            "b": (dp // 2) % side,
            "c": dp % 2,
            "z": lax.axis_index("seq"),
        }

    def rotate(self, x, axis):
        n = self.size[axis]
        if axis == "z":
            return lax.ppermute(x, "seq", [(i, (i + 1) % n) for i in range(n)])
        pairs = []
        side = self.size["b"]
        for i in range(self.n_dp):
            a, b, c = i // (2 * side), (i // 2) % side, i % 2
            if axis == "a":
                a = (a + 1) % n
            elif axis == "b":
                b = (b + 1) % n
            else:
                c = 1 - c
            pairs.append((i, (a * side + b) * 2 + c))
        return lax.ppermute(x, "dp", pairs)

    def zperm(self, x, pairs):
        return lax.ppermute(x, "seq", pairs)

    def same_core(self):
        return [list(range(c, self.n_dp, 2)) for c in range(2)]

    def ring(self, x, waits=()):
        parts = []
        for step in range(self.n_seq - 1):
            x = self.rotate(after(x, *waits[step]) if step < len(waits) else x, "z")
            parts.append(x)
        return parts

    def gather(self, x, axis, at=0):
        n, i = self.size[axis], self.index[axis]
        if n == 2:
            other = self.rotate(x, axis)
            return ordered(i == 0, x, other, at)
        parts = [x]
        for _ in range(n - 1):
            parts.append(self.rotate(parts[-1], axis))
        turned = jnp.stack(parts[::-1] + parts[::-1], 0)
        full = lax.dynamic_slice_in_dim(turned, n - 1 - i, n, 0)
        return jnp.moveaxis(full, 0, at)

    def scatter(self, x, axis, at=0, out=BF16):
        n, i = self.size[axis], self.index[axis]
        take = lambda k: lax.dynamic_index_in_dim(x, k, at, keepdims=False)
        if n == 2:
            other = self.rotate(take(1 - i), axis)
            return add(take(i), other, out)
        acc = take((i + n - 1) % n)
        for step in range(n - 1):
            got = self.rotate(acc, axis)
            last = step == n - 2
            acc = add(take((i + 2 * n - 2 - step) % n), got, out if last else BF16)
        return acc


def after(x, *others):
    others = [o for o in others if o is not None]
    return lax.optimization_barrier((x, *others))[0] if others else x


def add(x, y, out):
    return (x.astype(F32) + y.astype(F32)).astype(out)


def ordered(first, x, y, at):
    return jnp.stack([jnp.where(first, x, y), jnp.where(first, y, x)], at)


def z_gather(mv, w, waits=()):
    z, n = mv.index["z"], mv.n_seq
    blocks = [w] + mv.ring(w, waits)
    turned = jnp.stack(blocks[::-1] + blocks[::-1], 0)
    return lax.dynamic_slice_in_dim(turned, n - 1 - z, n, 0)


def small_plane(mv):
    return mv.size["a"] == 2 and mv.size["b"] == 2 and mv.n_seq == 4


def gather_core(mv, w, ready):
    k, rows, cols = w.shape
    c = mv.index["c"]
    full = lax.all_gather(w, "seq")
    zh = mv.n_seq // 2
    keep = lax.dynamic_slice_in_dim(full, c * zh, zh, 0)
    send = lax.dynamic_slice_in_dim(full, (1 - c) * zh, zh, 0)
    recv = mv.rotate(after(send, *ready), "c")
    block = ordered(c == 0, keep, recv, 2)
    return [block[j].reshape(k, 2 * rows, cols) for j in range(zh)]


GROUPS = ((0, 1), (2,))


def scatter_plane(mv, grad):
    quarter, k, rows, cols = grad.shape
    chips = mv.n_dp // 2
    x = grad
    if chips != quarter:
        x = jnp.moveaxis(grad, 1, 0).reshape(k, chips, quarter * rows // chips, cols)
        x = jnp.moveaxis(x, 0, 1)
    x = lax.psum_scatter(x, "dp", scatter_dimension=0, axis_index_groups=mv.same_core())
    x = x.reshape(k, 2, x.shape[1] // 2, cols)
    return x


def swap_cores(mv, x):
    c = mv.index["c"]
    take = lambda i: lax.dynamic_index_in_dim(x, i, 1, keepdims=False)
    return take(c), mv.rotate(take(1 - c), "c")


class ZSum:
    def __init__(self, mv, j, x):
        self.mv, self.j, self.x = mv, j, x

    def swap(self, wait):
        c = self.mv.index["c"]
        x = after(self.x, wait)
        take = lambda i: lax.dynamic_index_in_dim(x, i, 1, keepdims=False)
        mine, other = take(c), self.mv.rotate(take(1 - c), "c")
        here = (self.mv.index["z"] // 2) == c
        self.pair = mine, other
        self.near, self.far = jnp.where(here, mine, other), jnp.where(here, other, mine)
        return other

    def inwards(self, wait=None):
        got = self.mv.zperm(after(self.far, wait), [(0, 1), (3, 2)])
        self.far = add(self.far, got, BF16)
        return got

    def across(self, wait=None):
        got = self.mv.zperm(after(self.far, wait), [(1, 2), (2, 1)])
        self.near = add(self.near, got, BF16)
        return got

    def home(self, wait=None):
        j = self.j
        got = self.mv.zperm(after(self.near, wait), [(1 - j, j), (3 - j, 2 + j)])
        self.total = add(self.near, got, F32)
        return got


def z_totals(mv, sums):
    z, c = mv.index["z"], mv.index["c"]
    result = []
    for g in range(len(GROUPS)):
        units = [groups[g] for groups in sums]
        if mv.n_seq == 4:
            result.append(jnp.where(z % 2 == 0, units[0].total, units[1].total))
        else:
            full = jnp.stack([ordered(c == 0, *u.pair, 0) for u in units], 1)
            result.append(mv.scatter(full.reshape((mv.n_seq,) + units[0].pair[0].shape), "z", 0, F32))
    return result


def gather_small(mv, w):
    full = z_gather(mv, w)
    half = mv.n_seq // 2
    lo_one = mv.gather(full[:half], "b", 1)
    hi_one = mv.gather(full[half:], "a", 1)
    lo = mv.gather(lo_one, "a", 1)
    hi = mv.gather(hi_one, "b", 2)
    both = jnp.concatenate([lo, hi], 0)
    both = mv.gather(both, "c", 3)
    return both.reshape((mv.n_seq, mv.n_dp) + w.shape), (full, (lo_one, hi_one), (lo, hi))


def scatter_small(mv, g, between):
    na, nb = mv.size["a"], mv.size["b"]
    zs, _, rp, cols = g.shape
    x = g.reshape(zs, na, nb, 2, rp, cols)
    x = mv.scatter(x, "c", 3)
    half = zs // 2
    x = after(x, *between())
    lo = mv.scatter(mv.scatter(x[:half], "a", 1), "b", 1)
    hi = mv.scatter(mv.scatter(x[half:], "b", 2), "a", 1)
    x = jnp.concatenate([lo, hi], 0)
    return mv.scatter(x, "z", 0, F32), (lo, hi)


def reach_of(rows, n_seq):
    need, parts = MAX_DOC - 1, []
    while need > 0 and len(parts) + 1 < n_seq:
        parts.append(min(rows, -(-need // LANES) * LANES))
        need -= rows
    return parts


def halo(mv, x, waits=()):
    rows, n = x.shape[1], mv.n_seq
    left, right = [], []
    x_own = x
    for hop, cols in enumerate(reach_of(rows, n)):
        step = hop + 1
        if hop > 0:
            x = after(x, left[0], right[-1], *waits)
        left.insert(0, mv.zperm(x[:, rows - cols :], [(i, i + step) for i in range(n - step)]))
        right.append(mv.zperm(x[:, :cols], [(i + step, i) for i in range(n - step)]))
    return left + [x_own] + right


def dot(x, y, dims):
    return lax.dot_general(x, y, (dims, ((), ())), preferred_element_type=F32)


def nt(x, y):
    return dot(x, y, ((1,), (1,)))


def nn(x, y):
    return dot(x, y, ((1,), (0,)))


def tn(x, y):
    return dot(x, y, ((0,), (0,)))


def make_tiles(vec_ref, tiles):
    for h in range(HEADS):
        line = vec_ref[h : h + 1, :]
        wide = jnp.broadcast_to(line, (BLK, SPAN))
        rolled = pltpu.roll(wide, 0, 1, stride=1, stride_axis=0)
        tiles[h * 5] = jnp.broadcast_to(line[:, :1], (BLK, BLK))
        tiles[h * 5 + 4] = jnp.broadcast_to(line[:, SPAN - 1 :], (BLK, BLK))
        for d in (-1, 0, 1):
            at = SPAN // 2 + BLK * d
            tiles[h * 5 + 2 + d] = rolled[:, at : at + BLK]


def class_of(query_block, key_block):
    return jnp.clip(query_block - key_block, -2, 2) + 2


def lay_out(off, pieces, whole):
    middle = len(pieces) // 2
    at = off - sum(p.shape[1] for p in pieces[:middle])
    if at > 0:
        whole[:, :at] = jnp.zeros((whole.shape[0], at), whole.dtype)
    for p in pieces:
        whole[:, at : at + p.shape[1]] = p[...]
        at += p.shape[1]
    if at < whole.shape[1]:
        whole[:, at:] = jnp.zeros((whole.shape[0], whole.shape[1] - at), whole.dtype)


def block_at(k):
    return pl.ds(pl.multiple_of(k * BLK, BLK), BLK)


def forward_kernel(off, count, lohi, vec, q_ref, segq, segk, *rest):
    pieces = rest[:count]
    out, exact, lse, split, tiles, kv = rest[count:]
    i = pl.program_id(0)

    @pl.when(i == 0)
    def _():
        make_tiles(vec, tiles)
        lay_out(off, pieces, kv)

    own = off // BLK + i
    inner = HEADS * 64
    low, high = lohi[i, 0], lohi[i, 1]
    seg_row = segq[0]
    split[...] = jnp.zeros_like(split)
    lse[...] = jnp.zeros_like(lse)
    for pair in range(HEADS // 2):
        heads = (2 * pair, 2 * pair + 1)
        qs = [q_ref[h * 64 : h * 64 + 64, :] for h in heads]

        def body(kb, state):
            cols = block_at(kb)
            same = segk[cols, :] == seg_row
            kind = class_of(own, kb)
            new = []
            for e, h in enumerate(heads):
                peak, total, acc = state[e]
                s = tn(kv[h * 64 : h * 64 + 64, cols], qs[e]) + tiles[h * 5 + kind]
                s = jnp.where(same, s, MASKED)
                top = jnp.maximum(peak, jnp.max(s, axis=0, keepdims=True))
                fade = jnp.exp(peak - top)
                p = jnp.exp(s - top)
                total = total * fade + jnp.sum(p, axis=0, keepdims=True)
                acc = acc * fade + nn(kv[inner + h * 64 : inner + h * 64 + 64, cols], p.astype(BF16))
                new.append((top, total, acc))
            return tuple(new)

        start = (
            jnp.full((1, BLK), MASKED, F32),
            jnp.zeros((1, BLK), F32),
            jnp.zeros((64, BLK), F32),
        )
        state = lax.fori_loop(low, high, body, (start, start))
        for e, h in enumerate(heads):
            peak, total, acc = state[e]
            done = acc / total
            out[h * 64 : h * 64 + 64, :] = done.astype(BF16)
            exact[h * 64 : h * 64 + 64, :] = done
            log = peak + jnp.log(total)
            lse[h : h + 1, :] = log
            for part in range(3):
                piece = log.astype(BF16)
                split[part * 8 + h : part * 8 + h + 1, :] = piece
                log = log - piece.astype(F32)


def query_kernel(off, count, lohi, vec, q_ref, do_ref, lse, delta, segq, segk, *rest):
    pieces = rest[:count]
    dq, near, far, tiles, sums, kv = rest[count:]
    i = pl.program_id(0)

    @pl.when(i == 0)
    def _():
        make_tiles(vec, tiles)
        lay_out(off, pieces, kv)
        sums[...] = jnp.zeros_like(sums)

    own = off // BLK + i
    inner = HEADS * 64
    low, high = lohi[i, 0], lohi[i, 1]
    seg_row = segq[0]
    for pair in range(HEADS // 2):
        heads = (2 * pair, 2 * pair + 1)
        qs = [q_ref[h * 64 : h * 64 + 64, :] for h in heads]
        dos = [do_ref[h * 64 : h * 64 + 64, :] for h in heads]

        def body(kb, state):
            cols = block_at(kb)
            same = segk[cols, :] == seg_row
            kind = class_of(own, kb)
            new = []
            for e, h in enumerate(heads):
                keys = kv[h * 64 : h * 64 + 64, cols]
                s = tn(keys, qs[e]) + tiles[h * 5 + kind]
                s = jnp.where(same, s, MASKED)
                p = jnp.exp(s - lse[h : h + 1, :])
                dp = tn(kv[inner + h * 64 : inner + h * 64 + 64, cols], dos[e])
                ds = p * (dp - delta[h : h + 1, :])
                at = h * 5 + kind
                sums[at] = sums[at] + ds
                new.append(state[e] + nn(keys, ds.astype(BF16)))
            return tuple(new)

        start = jnp.zeros((64, BLK), F32)
        state = lax.fori_loop(low, high, body, (start, start))
        for e, h in enumerate(heads):
            dq[h * 64 : h * 64 + 64, :] = state[e].astype(BF16)

    @pl.when(i == pl.num_programs(0) - 1)
    def _():
        for h in range(HEADS):
            zero = jnp.zeros((BLK, BLK), F32)
            x = jnp.concatenate([sums[h * 5 + 1], sums[h * 5 + 2], sums[h * 5 + 3], zero], axis=1)
            n = BLK // 2
            while n >= 8:
                x = x[:n] + pltpu.roll(x[n:], SPAN - n, 1)
                n //= 2
            row = lax.broadcasted_iota(jnp.int32, x.shape, 0)
            for n in (4, 2, 1):
                x = jnp.where((row & n) != 0, pltpu.roll(x, SPAN - n, 1), x)
            near[h] = x
            far[h, 0] = jnp.sum(sums[h * 5].reshape(BLK // 8, 8, BLK), axis=0)
            far[h, 1] = jnp.sum(sums[h * 5 + 4].reshape(BLK // 8, 8, BLK), axis=0)


def key_kernel(off, count, lohi, vec, k_ref, v_ref, segq, segk, *rest):
    queries, answers = rest[:count], rest[count : 2 * count]
    dk, dv, tiles, qs, dos = rest[2 * count :]
    i = pl.program_id(0)

    @pl.when(i == 0)
    def _():
        make_tiles(vec, tiles)
        lay_out(off, queries, qs)
        lay_out(off, answers, dos)

    own = off // BLK + i
    inner = HEADS * 64
    low, high = lohi[i, 0], lohi[i, 1]
    seg_col = segk[...]
    for pair in range(HEADS // 2):
        heads = (2 * pair, 2 * pair + 1)
        ks = [k_ref[h * 64 : h * 64 + 64, :] for h in heads]
        vs = [v_ref[h * 64 : h * 64 + 64, :] for h in heads]

        def body(qb, state):
            cols = block_at(qb)
            same = seg_col == segq[qb]
            kind = class_of(qb, own)
            logs = qs[inner : inner + 8, cols].astype(F32)
            logs = logs + qs[inner + 8 : inner + 16, cols].astype(F32)
            logs = logs + qs[inner + 16 : inner + 24, cols].astype(F32)
            deltas = dos[inner : inner + 8, cols].astype(F32)
            deltas = deltas + dos[inner + 8 : inner + 16, cols].astype(F32)
            new = []
            for e, h in enumerate(heads):
                q, do = qs[h * 64 : h * 64 + 64, cols], dos[h * 64 : h * 64 + 64, cols]
                s = tn(ks[e], q) + tiles[h * 5 + kind]
                s = jnp.where(same, s, MASKED)
                p = jnp.exp(s - logs[h : h + 1, :])
                ds = p * (tn(vs[e], do) - deltas[h : h + 1, :])
                to_k, to_v = state[e]
                new.append((to_k + nt(q, ds.astype(BF16)), to_v + nt(do, p.astype(BF16))))
            return tuple(new)

        start = jnp.zeros((64, BLK), F32)
        state = lax.fori_loop(low, high, body, ((start, start), (start, start)))
        for e, h in enumerate(heads):
            dk[h * 64 : h * 64 + 64, :] = state[e][0].astype(BF16)
            dv[h * 64 : h * 64 + 64, :] = state[e][1].astype(BF16)


def whole_block(shape):
    return pl.BlockSpec(shape, lambda i: (0,) * len(shape))


def col_block(rows):
    return pl.BlockSpec((rows, BLK), lambda i: (0, i))


SMEM_SPEC = pl.BlockSpec(memory_space=pltpu.SMEM)
COL_SEGS = pl.BlockSpec((BLK, 1), lambda i: (i, 0))
ROW_SEGS = pl.BlockSpec((1, 1, BLK), lambda i: (i, 0, 0))
TILES = pltpu.VMEM((HEADS * 5, BLK, BLK), F32)
LIGHT = pl.CostEstimate(flops=10**9, bytes_accessed=8 * 2**20, transcendentals=0)


def params():
    return pltpu.CompilerParams(
        dimension_semantics=("arbitrary",), vmem_limit_bytes=VMEM_CAP
    )


def attend(off, span, lohi, vec, q, seg_row, seg_col, kv):
    inner, rows = q.shape
    return pl.pallas_call(
        partial(forward_kernel, off, len(kv)),
        grid=(rows // BLK,),
        in_specs=[SMEM_SPEC, whole_block(vec.shape), col_block(inner), ROW_SEGS, whole_block(seg_col.shape)]
        + [whole_block(p.shape) for p in kv],
        out_specs=[col_block(inner), col_block(inner), col_block(8), col_block(32)],
        out_shape=[
            jax.ShapeDtypeStruct((inner, rows), BF16),
            jax.ShapeDtypeStruct((inner, rows), F32),
            jax.ShapeDtypeStruct((8, rows), F32),
            jax.ShapeDtypeStruct((32, rows), BF16),
        ],
        scratch_shapes=[TILES, pltpu.VMEM((2 * inner, span), BF16)],
        cost_estimate=LIGHT,
        name="attend",
        compiler_params=params(),
    )(lohi, vec, q, seg_row, seg_col, *kv)


def attend_queries(off, span, lohi, vec, q, do, lse, delta, seg_row, seg_col, kv):
    inner, rows = q.shape
    return pl.pallas_call(
        partial(query_kernel, off, len(kv)),
        grid=(rows // BLK,),
        in_specs=[
            SMEM_SPEC,
            whole_block(vec.shape),
            col_block(inner),
            col_block(inner),
            col_block(8),
            col_block(8),
            ROW_SEGS,
            whole_block(seg_col.shape),
        ]
        + [whole_block(p.shape) for p in kv],
        out_specs=[
            col_block(inner),
            whole_block((HEADS, 8, SPAN)),
            whole_block((HEADS, 2, 8, BLK)),
        ],
        out_shape=[
            jax.ShapeDtypeStruct((inner, rows), BF16),
            jax.ShapeDtypeStruct((HEADS, 8, SPAN), F32),
            jax.ShapeDtypeStruct((HEADS, 2, 8, BLK), F32),
        ],
        scratch_shapes=[TILES, TILES, pltpu.VMEM((2 * inner, span), BF16)],
        cost_estimate=LIGHT,
        name="attend_queries",
        compiler_params=params(),
    )(lohi, vec, q, do, lse, delta, seg_row, seg_col, *kv)


def attend_keys(off, span, lohi, vec, k, v, seg_row, seg_col, queries, answers):
    inner, rows = k.shape
    both = list(queries) + list(answers)
    return pl.pallas_call(
        partial(key_kernel, off, len(queries)),
        grid=(rows // BLK,),
        in_specs=[
            SMEM_SPEC,
            whole_block(vec.shape),
            col_block(inner),
            col_block(inner),
            whole_block(seg_row.shape),
            COL_SEGS,
        ]
        + [whole_block(p.shape) for p in both],
        out_specs=[col_block(inner), col_block(inner)],
        out_shape=[jax.ShapeDtypeStruct((inner, rows), BF16)] * 2,
        scratch_shapes=[
            TILES,
            pltpu.VMEM((queries[0].shape[0], span), BF16),
            pltpu.VMEM((answers[0].shape[0], span), BF16),
        ],
        cost_estimate=LIGHT,
        name="attend_keys",
        compiler_params=params(),
    )(lohi, vec, k, v, seg_row, seg_col, *both)


def ffn_kernel(nm, half, count, order, na, nb, ca, cb, nat, nbt, cat, cbt, *rest):
    pieces = rest[:count]
    out_a, out_b, gn_a, gn_b, *grads = rest[count : count + 4 + len(GROUPS)]
    weights, x, ct, hid, ggr, gur, sem = rest[count + 4 + len(GROUPS) :]
    i = pl.program_id(0)

    @pl.when(i == 0)
    def _():
        copies = []
        for piece in pieces:
            rows = piece.shape[2]
            for n in range(piece.shape[0]):
                k = len(copies) // 3
                at = pl.multiple_of(order[k], 16)
                for m in range(3):
                    copies.append(
                        pltpu.make_async_copy(
                            piece.at[n, m], weights.at[m, pl.ds(at, rows), :], sem.at[k, m]
                        )
                    )
        for copy in copies:
            copy.start()
        for copy in copies:
            copy.wait()

    @pl.when(i < half)
    def _():
        x[...] = na[...].T
        ct[...] = ca[...].T

    @pl.when((i >= half) & (i < nm))
    def _():
        x[...] = nb[...].T
        ct[...] = cb[...].T

    @pl.when(i < nm)
    def _():
        rows = pl.ds(pl.multiple_of(i * BLK, BLK), BLK)
        g = nn(x[...], weights[0])
        u = nn(x[...], weights[1])
        gh = nn(ct[...], weights[2])
        square = g * g
        t = jnp.tanh(GELU_K * g * (1.0 + GELU_A * square))
        part = 0.5 * (1.0 + t)
        gelu = g * part
        slope = part + 0.5 * g * (1.0 - t * t) * (GELU_K * (1.0 + 3.0 * GELU_A * square))
        h = (gelu * u).astype(BF16)
        gg = (gh * u * slope).astype(BF16)
        gu = (gh * gelu).astype(BF16)
        hid[rows, :] = h
        ggr[rows, :] = gg
        gur[rows, :] = gu
        out = nt(weights[2], h).astype(BF16)
        gn = (nt(weights[0], gg) + nt(weights[1], gu)).astype(BF16)

        @pl.when(i < half)
        def _():
            out_a[...] = out
            gn_a[...] = gn

        @pl.when(i >= half)
        def _():
            out_b[...] = out
            gn_b[...] = gn

    @pl.when(i >= nm)
    def _():
        t = hid.shape[0] // 2

        def product(first, second, right):
            return (nn(first[...], right[:t, :]) + nn(second[...], right[t:, :])).astype(BF16)

        lefts = ((nat, nbt, ggr), (nat, nbt, gur), (cat, cbt, hid))
        for g, members in enumerate(GROUPS):
            for n, m in enumerate(members):
                grads[g][0, n] = product(*lefts[m])


def ffn(n_own, n_other, c_own, c_other, pieces, starts):
    depth, t = n_own.shape
    cols = pieces[0].shape[3]
    half = t // BLK
    nm = 2 * half
    tile = depth // 4
    scalars = jnp.stack([jnp.asarray(v, jnp.int32) for v in starts])
    own = pl.BlockSpec((depth, BLK), lambda i, o: (0, jnp.minimum(i, half - 1)))
    other = pl.BlockSpec((depth, BLK), lambda i, o: (0, jnp.clip(i - half, 0, half - 1)))
    later = pl.BlockSpec((tile, t), lambda i, o: (jnp.maximum(i - nm, 0), 0))
    place = pl.BlockSpec(memory_space=pl.ANY)
    grads = [
        pl.BlockSpec((1, len(m), tile, cols), lambda i, o: (jnp.maximum(i - nm, 0), 0, 0, 0)) for m in GROUPS
    ]
    return pl.pallas_call(
        partial(ffn_kernel, nm, half, len(pieces)),
        grid_spec=pltpu.PrefetchScalarGridSpec(
            num_scalar_prefetch=1,
            grid=(nm + 4,),
            in_specs=[own, other, own, other, later, later, later, later] + [place] * len(pieces),
            out_specs=[own, other, own, other] + grads,
            scratch_shapes=[
                pltpu.VMEM((3, depth, cols), BF16),
                pltpu.VMEM((BLK, depth), BF16),
                pltpu.VMEM((BLK, depth), BF16),
                pltpu.VMEM((2 * t, cols), BF16),
                pltpu.VMEM((2 * t, cols), BF16),
                pltpu.VMEM((2 * t, cols), BF16),
                pltpu.SemaphoreType.DMA((len(starts), 3)),
            ],
        ),
        out_shape=[jax.ShapeDtypeStruct((depth, t), BF16)] * 4
        + [jax.ShapeDtypeStruct((4, len(m), tile, cols), BF16) for m in GROUPS],
        cost_estimate=LIGHT,
        name="ffn",
        compiler_params=params(),
    )(scalars, n_own, n_other, c_own, c_other, n_own, n_other, c_own, c_other, *pieces)


def rms_scale(x):
    return lax.rsqrt(jnp.mean(x * x, axis=0, keepdims=True) + EPS)


def norm_back(grad, x, scale, gain):
    gain_grad = jnp.sum(grad * (x * scale), axis=1)
    weighted = grad * gain
    dots = jnp.mean(weighted * x, axis=0, keepdims=True)
    return scale * weighted - x * (scale * scale * scale * dots), gain_grad


def on_device(
    n_dp,
    n_seq,
    inputs,
    segments,
    cotangent,
    w_query,
    w_key,
    w_value,
    w_out,
    w_gate,
    w_up,
    w_down,
    gain_attn,
    gain_ffn,
    rel_table,
):
    mv = Moves(n_dp, n_seq)
    seqs, rows, depth = inputs.shape
    source = inputs.reshape(seqs * rows, depth).T.astype(F32)
    tangent = cotangent.reshape(seqs * rows, depth).T
    rw, sc = w_query.shape
    inner = sc * n_seq
    wide = 4 * sc
    seg_rows = -(-rows // wide)
    rp = -(-(rw + 2 + seg_rows) // 16) * 16

    body = jnp.concatenate([w_query, w_key, w_value, w_out.T], axis=1)
    table_row = rel_table.reshape(-1)
    pad_to = lambda v: jnp.pad(v, (0, -v.shape[0] % wide)).reshape(-1, wide)
    packed = jnp.concatenate(
        [
            body,
            pad_to(jnp.concatenate([gain_attn, gain_ffn])),
            pad_to(table_row),
            pad_to(segments.reshape(rows).astype(BF16)),
            jnp.zeros((rp - rw - 2 - seg_rows, wide), BF16),
        ],
        axis=0,
    )
    att, stages = gather_small(mv, packed)
    full = att[:, :, :rw, :].reshape(n_seq, depth, wide)
    gain_one = att[0, :, rw, :rw].reshape(depth, 1).astype(F32)
    gain_two = att[0, :, rw, rw : 2 * rw].reshape(depth, 1).astype(F32)
    table = att[0, :, rw + 1, : table_row.shape[0]].reshape(BUCKETS, HEADS)
    here = lax.dynamic_index_in_dim(att, lax.axis_index("dp"), 1, keepdims=False)
    seg_seq = here[:, rw + 2 : rw + 2 + seg_rows, :].reshape(n_seq, -1)[:, :rows].astype(jnp.int32)

    scale_one = rms_scale(source)
    normed = ((source * scale_one) * gain_one).astype(BF16)
    qkv = jnp.einsum("zdc,dt->zct", full[:, :, : 3 * sc], normed, preferred_element_type=F32)
    qkv = jnp.transpose(qkv.astype(BF16).reshape(n_seq, 3, sc, rows), (1, 0, 2, 3))
    q = qkv[0].reshape(inner, rows)
    k = qkv[1].reshape(inner, rows)
    v = qkv[2].reshape(inner, rows)

    zh = n_seq // 2
    small = small_plane(mv)
    tangent_other = mv.rotate(tangent, "c")
    cores = gather_core(mv, jnp.stack([w_gate, w_up, w_down.T]), (q, tangent_other))
    kv_halo = halo(mv, after(jnp.concatenate([k, v], 0), cores[0]))
    pieces, starts = [], []
    for j in range(zh):
        full_block = lax.all_gather(cores[j], "dp", axis_index_groups=mv.same_core())
        if small:
            pieces.append([full_block])
            starts.append([jnp.int32(2 * rw * k) for k in range(4)])
        else:
            pieces.append([jnp.moveaxis(full_block, 0, 1).reshape(1, 3, depth, -1)])
            starts.append([jnp.int32(0)])

    off = -(-MAX_DOC // BLK) * BLK
    span = 2 * off + rows
    blocks = span // BLK
    seg_own = segments.reshape(rows)
    line = jnp.pad(seg_seq.reshape(-1), (off, off), constant_values=-1)
    seg_all = lax.dynamic_slice_in_dim(line, mv.index["z"] * rows, span, 0)
    seg_row = seg_all.reshape(blocks, 1, BLK)
    seg_col = seg_all.reshape(span, 1)
    own_row = seg_own.reshape(rows // BLK, 1, BLK)
    own_col = seg_own.reshape(rows, 1)
    spots = jnp.arange(span, dtype=jnp.int32)
    firsts = seg_own[::BLK]
    lasts = seg_own[BLK - 1 :: BLK]
    low = jnp.min(jnp.where(seg_all[None] == firsts[:, None], spots[None], 1 << 20), axis=1) // BLK
    high = jnp.max(jnp.where(seg_all[None] == lasts[:, None], spots[None], -1), axis=1) // BLK + 1
    lohi = jnp.stack([low, high], 1).astype(jnp.int32)

    buckets = bucket_table()
    buckets = np.concatenate([buckets[-1:], buckets[:0:-1]])
    chosen = jnp.asarray((buckets[:, None] == np.arange(BUCKETS)[None, :]), BF16)
    vec = dot(table, chosen, ((0,), (1,)))

    attended, exact, lse, lse_parts = attend(
        off, span, lohi, vec, q, own_row, seg_col, kv_halo
    )
    q_halo = halo(mv, jnp.concatenate([q, lse_parts], 0))

    mixed = source + jnp.einsum(
        "zdc,zct->dt", full[:, :, 3 * sc :], attended.reshape(n_seq, sc, rows), preferred_element_type=F32
    )
    scale_two = rms_scale(mixed)
    normed_two = ((mixed * scale_two) * gain_two).astype(BF16)

    normed_other = mv.rotate(normed_two, "c")
    parts, sums = [], []
    for j in range(zh):
        results = ffn(
            after(normed_two, *(parts[-1] if j else q_halo)),
            normed_other,
            tangent,
            tangent_other,
            pieces[j],
            starts[j],
        )
        parts.append(results[:4])
        sums.append([ZSum(mv, j, scatter_plane(mv, grad)) for grad in results[4:]])
    out_own, out_other, gn_own, gn_other = (
        sum(four[m].astype(F32) for four in parts) for m in range(4)
    )
    gn_recv = mv.rotate(gn_other.astype(BF16), "c")
    grad_n2 = gn_own + gn_recv.astype(F32)

    grad_mixed, grad_gain_two = norm_back(grad_n2, mixed, scale_two, gain_two)
    grad_mixed = grad_mixed + tangent.astype(F32)
    grad_branch = grad_mixed.astype(BF16)
    grad_att = jnp.einsum(
        "zdc,dt->zct", full[:, :, 3 * sc :], grad_branch, preferred_element_type=F32
    )
    grad_att = grad_att.reshape(inner, rows).astype(BF16)
    delta = jnp.sum((grad_att.astype(F32) * exact).reshape(HEADS, inner // HEADS, rows), axis=1)
    delta = jnp.pad(delta, ((0, 8 - HEADS), (0, 0)))
    delta_top = lax.reduce_precision(delta, 8, 7)
    answers = jnp.concatenate([grad_att, delta_top.astype(BF16), (delta - delta_top).astype(BF16)], 0)
    do_halo = halo(mv, answers)

    dq, near, far = attend_queries(
        off, span, lohi, vec, q, grad_att, lse, delta, own_row, seg_col, kv_halo
    )
    out_recv = mv.rotate(after(out_other.astype(BF16), dq), "c")
    outputs = (mixed + out_own + out_recv.astype(F32)).astype(BF16)
    swaps = [u.swap(dq) for u in sums[0]]
    k_then = after(k, dq, *swaps)
    dk, dv = attend_keys(off, span, lohi, vec, k_then, v, seg_row, own_col, q_halo, do_halo)
    if small:
        dk = after(dk, *[u.inwards() for u in sums[0]])

    sheared = jnp.roll(jnp.sum(near, axis=1), BLK, axis=1)
    grad_table = jnp.dot(sheared, chosen.astype(F32), precision=lax.Precision.HIGHEST).T
    far_sums = jnp.sum(far, axis=(2, 3))
    grad_table = grad_table.at[31].add(far_sums[:, 0]).at[15].add(far_sums[:, 1])

    for groups in sums[1:]:
        swaps = [u.swap(dk) for u in groups]

    split = lambda x: x.reshape(n_seq, sc, rows)
    rows_z = jnp.concatenate([split(dq), split(dk), split(dv)], axis=1)
    grad_normed = jnp.einsum(
        "zdc,zct->dt", full[:, :, : 3 * sc], rows_z, preferred_element_type=F32
    )
    grad_source, grad_gain_one = norm_back(grad_normed, source, scale_one, gain_one)
    input_grad = (grad_mixed + grad_source).astype(BF16)

    g_in = jnp.einsum("dt,zct->zdc", normed, rows_z, preferred_element_type=F32)
    g_out = jnp.einsum("dt,zct->zdc", grad_branch, split(attended), preferred_element_type=F32)
    grads = jnp.concatenate([g_in, g_out], axis=2).reshape(n_seq, n_dp, rw, wide)
    gain_rows = jnp.concatenate(
        [grad_gain_one.reshape(n_dp, rw), grad_gain_two.reshape(n_dp, rw)], axis=1
    )
    widen = lambda x: jnp.broadcast_to(
        jnp.pad(x, ((0, 0), (0, wide - x.shape[1])))[None, :, None, :], (n_seq, n_dp, 1, wide)
    )
    grads = jnp.concatenate(
        [
            grads,
            widen(gain_rows),
            widen(grad_table.reshape(n_dp, -1)),
            jnp.zeros((n_seq, n_dp, rp - rw - 2, wide), F32),
        ],
        axis=2,
    ).astype(BF16)
    if small:
        grads = after(grads, *[u.across() for u in sums[0]])
    own, stages = scatter_small(mv, grads, lambda: [u.home() for u in sums[0]] + swaps if small else [])
    if small:
        for step in (ZSum.inwards, ZSum.across, ZSum.home):
            for u in sums[1]:
                step(u)
    own_ffn = z_totals(mv, sums)

    return (
        outputs.T.reshape(seqs, rows, depth),
        input_grad.T.reshape(seqs, rows, depth),
        own[:rw, :sc],
        own[:rw, sc : 2 * sc],
        own[:rw, 2 * sc : 3 * sc],
        own[:rw, 3 * sc :].T,
        own_ffn[0][0],
        own_ffn[0][1],
        own_ffn[1][0].T,
        own[rw, :rw],
        own[rw, rw : 2 * rw],
        own[rw + 1, : table_row.shape[0]].reshape(rel_table.shape),
    )


def solution(mesh):
    row, col = P("dp", "seq"), P("seq", "dp")
    tokens = P("dp", "seq", None)
    return jax.shard_map(
        partial(on_device, mesh.shape["dp"], mesh.shape["seq"]),
        mesh=mesh,
        in_specs=(tokens, row, tokens, row, row, row, col, row, row, col, P("dp"), P("dp"), P("dp", None)),
        out_specs=(tokens, tokens, row, row, row, col, row, row, col, P("dp"), P("dp"), P("dp", None)),
        check_vma=False,
    )
```

```python
import math
from functools import partial

import jax
import jax.numpy as jnp
import numpy as np
from jax import lax
from jax.experimental import pallas as pl
from jax.experimental.pallas import tpu as pltpu
from jax.sharding import PartitionSpec as P

HEADS = 6
BUCKETS = 32
MAX_DOC = 800
BLK = 256
SPAN = 1024
EPS = 1e-06
MASKED = -1e30
F32 = jnp.float32
BF16 = jnp.bfloat16
VMEM_CAP = 58 * 1024 * 1024
LANES = 128
GELU_K = math.sqrt(2.0 / math.pi)
GELU_A = 0.044715


def bucket_table():
    relative = np.arange(SPAN) - SPAN // 2
    distance = np.abs(relative)
    steps = np.array([12, 16, 23, 32, 46, 64, 91])
    levels = (distance[:, None] >= steps[None, :]).sum(axis=1)
    inside = np.where(distance < 8, distance, 8 + levels)
    return (inside + 16 * (relative > 0)).astype(np.int32)


class Moves:
    def __init__(self, n_dp, n_seq):
        self.n_dp, self.n_seq = n_dp, n_seq
        plane = n_dp // 2
        side = int(round(math.sqrt(plane)))
        self.size = {"a": plane // side, "b": side, "c": 2, "z": n_seq}
        dp = lax.axis_index("dp")
        self.last = {}
        self.index = {
            "a": dp // (2 * side),
            "b": (dp // 2) % side,
            "c": dp % 2,
            "z": lax.axis_index("seq"),
        }

    def rotate(self, x, axis):
        n = self.size[axis]
        if axis == "z":
            return lax.ppermute(x, "seq", [(i, (i + 1) % n) for i in range(n)])
        pairs = []
        side = self.size["b"]
        for i in range(self.n_dp):
            a, b, c = i // (2 * side), (i // 2) % side, i % 2
            if axis == "a":
                a = (a + 1) % n
            elif axis == "b":
                b = (b + 1) % n
            else:
                c = 1 - c
            pairs.append((i, (a * side + b) * 2 + c))
        return lax.ppermute(x, "dp", pairs)

    def zperm(self, x, pairs):
        return lax.ppermute(x, "seq", pairs)

    def same_core(self):
        return [list(range(c, self.n_dp, 2)) for c in range(2)]

    def ring(self, x, waits=()):
        parts = []
        for step in range(self.n_seq - 1):
            x = self.rotate(after(x, *waits[step]) if step < len(waits) else x, "z")
            parts.append(x)
        return parts

    def gather(self, x, axis, at=0):
        n, i = self.size[axis], self.index[axis]
        if n == 2:
            other = self.rotate(x, axis)
            return ordered(i == 0, x, other, at)
        parts = [x]
        for _ in range(n - 1):
            parts.append(self.rotate(parts[-1], axis))
        turned = jnp.stack(parts[::-1] + parts[::-1], 0)
        full = lax.dynamic_slice_in_dim(turned, n - 1 - i, n, 0)
        return jnp.moveaxis(full, 0, at)

    def scatter(self, x, axis, at=0, out=BF16):
        n, i = self.size[axis], self.index[axis]
        take = lambda k: lax.dynamic_index_in_dim(x, k, at, keepdims=False)
        if n == 2:
            other = self.rotate(take(1 - i), axis)
            return add(take(i), other, out)
        acc = take((i + n - 1) % n)
        for step in range(n - 1):
            got = self.rotate(acc, axis)
            last = step == n - 2
            acc = add(take((i + 2 * n - 2 - step) % n), got, out if last else BF16)
        return acc


def after(x, *others):
    others = [o for o in others if o is not None]
    return lax.optimization_barrier((x, *others))[0] if others else x


def add(x, y, out):
    return (x.astype(F32) + y.astype(F32)).astype(out)


def ordered(first, x, y, at):
    return jnp.stack([jnp.where(first, x, y), jnp.where(first, y, x)], at)


def z_gather(mv, w, waits=()):
    z, n = mv.index["z"], mv.n_seq
    blocks = [w] + mv.ring(w, waits)
    turned = jnp.stack(blocks[::-1] + blocks[::-1], 0)
    return lax.dynamic_slice_in_dim(turned, n - 1 - z, n, 0)


def small_plane(mv):
    return mv.size["a"] == 2 and mv.size["b"] == 2 and mv.n_seq == 4


def gather_core(mv, w, ready):
    k, rows, cols = w.shape
    c = mv.index["c"]
    full = lax.all_gather(w, "seq")
    zh = mv.n_seq // 2
    keep = lax.dynamic_slice_in_dim(full, c * zh, zh, 0)
    send = lax.dynamic_slice_in_dim(full, (1 - c) * zh, zh, 0)
    recv = mv.rotate(after(send, *ready), "c")
    block = ordered(c == 0, keep, recv, 2)
    return [block[j].reshape(k, 2 * rows, cols) for j in range(zh)]


def scatter_plane(mv, grad):
    quarter, k, rows, cols = grad.shape
    chips = mv.n_dp // 2
    x = grad
    if chips != quarter:
        x = jnp.moveaxis(grad, 1, 0).reshape(k, chips, quarter * rows // chips, cols)
        x = jnp.moveaxis(x, 0, 1)
    x = lax.psum_scatter(x, "dp", scatter_dimension=0, axis_index_groups=mv.same_core())
    x = x.reshape(k, 2, x.shape[1] // 2, cols)
    return x


def swap_cores(mv, x):
    c = mv.index["c"]
    take = lambda i: lax.dynamic_index_in_dim(x, i, 1, keepdims=False)
    return take(c), mv.rotate(take(1 - c), "c")


class ZSum:
    def __init__(self, mv, j, x):
        self.mv, self.j, self.x = mv, j, x

    def swap(self, wait):
        c = self.mv.index["c"]
        x = after(self.x, wait)
        take = lambda i: lax.dynamic_index_in_dim(x, i, 1, keepdims=False)
        mine, other = take(c), self.mv.rotate(take(1 - c), "c")
        here = (self.mv.index["z"] // 2) == c
        self.pair = mine, other
        self.near, self.far = jnp.where(here, mine, other), jnp.where(here, other, mine)
        return other

    def inwards(self, wait=None):
        got = self.mv.zperm(after(self.far, wait), [(0, 1), (3, 2)])
        self.far = add(self.far, got, BF16)
        return got

    def across(self, wait=None):
        got = self.mv.zperm(after(self.far, wait), [(1, 2), (2, 1)])
        self.near = add(self.near, got, BF16)
        return got

    def home(self, wait=None):
        j = self.j
        got = self.mv.zperm(after(self.near, wait), [(1 - j, j), (3 - j, 2 + j)])
        self.total = add(self.near, got, F32)
        return got


def z_totals(mv, sums):
    z, c = mv.index["z"], mv.index["c"]
    join = lambda parts: jnp.concatenate(parts, 0)
    if mv.n_seq == 4:
        first, second = (join([u.total for u in units]) for units in sums)
        return jnp.where(z % 2 == 0, first, second)
    full = jnp.stack(
        [ordered(c == 0, *(join([u.pair[i] for u in units]) for i in range(2)), 0) for units in sums], 1
    )
    return mv.scatter(full.reshape((mv.n_seq,) + full.shape[2:]), "z", 0, F32)


def gather_small(mv, w):
    full = z_gather(mv, w)
    half = mv.n_seq // 2
    lo_one = mv.gather(full[:half], "b", 1)
    hi_one = mv.gather(full[half:], "a", 1)
    lo = mv.gather(lo_one, "a", 1)
    hi = mv.gather(hi_one, "b", 2)
    both = jnp.concatenate([lo, hi], 0)
    both = mv.gather(both, "c", 3)
    return both.reshape((mv.n_seq, mv.n_dp) + w.shape), (full, (lo_one, hi_one), (lo, hi))


def scatter_small(mv, g, before_plane, midway, before_z):
    na, nb = mv.size["a"], mv.size["b"]
    zs, _, rp, cols = g.shape
    x = g.reshape(zs, na, nb, 2, rp, cols)
    x = mv.scatter(x, "c", 3)
    half = zs // 2
    x = after(x, *before_plane(x))
    waits = midway(x)
    lo = mv.scatter(x[:half], "a", 1)
    hi = mv.scatter(x[half:], "b", 2)
    lo = mv.scatter(after(lo, *waits), "b", 1)
    hi = mv.scatter(after(hi, *waits), "a", 1)
    x = jnp.concatenate([lo, hi], 0)
    return mv.scatter(after(x, *before_z(x)), "z", 0, F32)


def reach_of(rows, n_seq):
    need, parts = MAX_DOC - 1, []
    while need > 0 and len(parts) + 1 < n_seq:
        parts.append(min(rows, -(-need // LANES) * LANES))
        need -= rows
    return parts


def halo(mv, x, chained=True):
    rows, n = x.shape[1], mv.n_seq
    left, right = [], []
    own = x
    for hop, cols in enumerate(reach_of(rows, n)):
        step = hop + 1
        if chained and hop > 0:
            x = after(x, left[0], right[-1])
        left.insert(0, mv.zperm(x[:, rows - cols :], [(i, i + step) for i in range(n - step)]))
        right.append(mv.zperm(x[:, :cols], [(i + step, i) for i in range(n - step)]))
    return left + [own] + right


def dot(x, y, dims):
    return lax.dot_general(x, y, (dims, ((), ())), preferred_element_type=F32)


def nt(x, y):
    return dot(x, y, ((1,), (1,)))


def nn(x, y):
    return dot(x, y, ((1,), (0,)))


def tn(x, y):
    return dot(x, y, ((0,), (0,)))


def make_tiles(vec_ref, tiles):
    for h in range(HEADS):
        line = vec_ref[h : h + 1, :]
        wide = jnp.broadcast_to(line, (BLK, SPAN))
        rolled = pltpu.roll(wide, 0, 1, stride=1, stride_axis=0)
        tiles[h * 5] = jnp.broadcast_to(line[:, :1], (BLK, BLK))
        tiles[h * 5 + 4] = jnp.broadcast_to(line[:, SPAN - 1 :], (BLK, BLK))
        for d in (-1, 0, 1):
            at = SPAN // 2 + BLK * d
            tiles[h * 5 + 2 + d] = rolled[:, at : at + BLK]


def class_of(query_block, key_block):
    return jnp.clip(query_block - key_block, -2, 2) + 2


def lay_out(off, pieces, whole):
    middle = len(pieces) // 2
    at = off - sum(p.shape[1] for p in pieces[:middle])
    if at > 0:
        whole[:, :at] = jnp.zeros((whole.shape[0], at), whole.dtype)
    for p in pieces:
        whole[:, at : at + p.shape[1]] = p[...]
        at += p.shape[1]
    if at < whole.shape[1]:
        whole[:, at:] = jnp.zeros((whole.shape[0], whole.shape[1] - at), whole.dtype)


def block_at(k):
    return pl.ds(pl.multiple_of(k * BLK, BLK), BLK)


def forward_kernel(off, count, lohi, vec, q_ref, segq, segk, *rest):
    pieces = rest[:count]
    out, exact, lse, split, tiles, kv = rest[count:]
    i = pl.program_id(0)

    @pl.when(i == 0)
    def _():
        make_tiles(vec, tiles)
        lay_out(off, pieces, kv)

    own = off // BLK + i
    inner = HEADS * 64
    low, high = lohi[i, 0], lohi[i, 1]
    seg_row = segq[0]
    split[...] = jnp.zeros_like(split)
    lse[...] = jnp.zeros_like(lse)
    for pair in range(HEADS // 2):
        heads = (2 * pair, 2 * pair + 1)
        qs = [q_ref[h * 64 : h * 64 + 64, :] for h in heads]

        def body(kb, state):
            cols = block_at(kb)
            same = segk[cols, :] == seg_row
            kind = class_of(own, kb)
            new = []
            for e, h in enumerate(heads):
                peak, total, acc = state[e]
                s = tn(kv[h * 64 : h * 64 + 64, cols], qs[e]) + tiles[h * 5 + kind]
                s = jnp.where(same, s, MASKED)
                top = jnp.maximum(peak, jnp.max(s, axis=0, keepdims=True))
                fade = jnp.exp(peak - top)
                p = jnp.exp(s - top)
                total = total * fade + jnp.sum(p, axis=0, keepdims=True)
                acc = acc * fade + nn(kv[inner + h * 64 : inner + h * 64 + 64, cols], p.astype(BF16))
                new.append((top, total, acc))
            return tuple(new)

        start = (
            jnp.full((1, BLK), MASKED, F32),
            jnp.zeros((1, BLK), F32),
            jnp.zeros((64, BLK), F32),
        )
        state = lax.fori_loop(low, high, body, (start, start))
        for e, h in enumerate(heads):
            peak, total, acc = state[e]
            done = acc / total
            out[h * 64 : h * 64 + 64, :] = done.astype(BF16)
            exact[h * 64 : h * 64 + 64, :] = done
            log = peak + jnp.log(total)
            lse[h : h + 1, :] = log
            for part in range(3):
                piece = log.astype(BF16)
                split[part * 8 + h : part * 8 + h + 1, :] = piece
                log = log - piece.astype(F32)


def query_kernel(off, count, lohi, vec, q_ref, do_ref, lse, delta, segq, segk, *rest):
    pieces = rest[:count]
    dq, near, far, tiles, sums, kv = rest[count:]
    i = pl.program_id(0)

    @pl.when(i == 0)
    def _():
        make_tiles(vec, tiles)
        lay_out(off, pieces, kv)
        sums[...] = jnp.zeros_like(sums)

    own = off // BLK + i
    inner = HEADS * 64
    low, high = lohi[i, 0], lohi[i, 1]
    seg_row = segq[0]
    for pair in range(HEADS // 2):
        heads = (2 * pair, 2 * pair + 1)
        qs = [q_ref[h * 64 : h * 64 + 64, :] for h in heads]
        dos = [do_ref[h * 64 : h * 64 + 64, :] for h in heads]

        def body(kb, state):
            cols = block_at(kb)
            same = segk[cols, :] == seg_row
            kind = class_of(own, kb)
            new = []
            for e, h in enumerate(heads):
                keys = kv[h * 64 : h * 64 + 64, cols]
                s = tn(keys, qs[e]) + tiles[h * 5 + kind]
                s = jnp.where(same, s, MASKED)
                p = jnp.exp(s - lse[h : h + 1, :])
                dp = tn(kv[inner + h * 64 : inner + h * 64 + 64, cols], dos[e])
                ds = p * (dp - delta[h : h + 1, :])
                at = h * 5 + kind
                sums[at] = sums[at] + ds
                new.append(state[e] + nn(keys, ds.astype(BF16)))
            return tuple(new)

        start = jnp.zeros((64, BLK), F32)
        state = lax.fori_loop(low, high, body, (start, start))
        for e, h in enumerate(heads):
            dq[h * 64 : h * 64 + 64, :] = state[e].astype(BF16)

    @pl.when(i == pl.num_programs(0) - 1)
    def _():
        for h in range(HEADS):
            zero = jnp.zeros((BLK, BLK), F32)
            x = jnp.concatenate([sums[h * 5 + 1], sums[h * 5 + 2], sums[h * 5 + 3], zero], axis=1)
            n = BLK // 2
            while n >= 8:
                x = x[:n] + pltpu.roll(x[n:], SPAN - n, 1)
                n //= 2
            row = lax.broadcasted_iota(jnp.int32, x.shape, 0)
            for n in (4, 2, 1):
                x = jnp.where((row & n) != 0, pltpu.roll(x, SPAN - n, 1), x)
            near[h] = x
            far[h, 0] = jnp.sum(sums[h * 5].reshape(BLK // 8, 8, BLK), axis=0)
            far[h, 1] = jnp.sum(sums[h * 5 + 4].reshape(BLK // 8, 8, BLK), axis=0)


def key_kernel(off, count, lohi, vec, k_ref, v_ref, segq, segk, *rest):
    queries, answers = rest[:count], rest[count : 2 * count]
    dk, dv, tiles, qs, dos = rest[2 * count :]
    i = pl.program_id(0)

    @pl.when(i == 0)
    def _():
        make_tiles(vec, tiles)
        lay_out(off, queries, qs)
        lay_out(off, answers, dos)

    own = off // BLK + i
    inner = HEADS * 64
    low, high = lohi[i, 0], lohi[i, 1]
    seg_col = segk[...]
    for pair in range(HEADS // 2):
        heads = (2 * pair, 2 * pair + 1)
        ks = [k_ref[h * 64 : h * 64 + 64, :] for h in heads]
        vs = [v_ref[h * 64 : h * 64 + 64, :] for h in heads]

        def body(qb, state):
            cols = block_at(qb)
            same = seg_col == segq[qb]
            kind = class_of(qb, own)
            logs = qs[inner : inner + 8, cols].astype(F32)
            logs = logs + qs[inner + 8 : inner + 16, cols].astype(F32)
            logs = logs + qs[inner + 16 : inner + 24, cols].astype(F32)
            deltas = dos[inner : inner + 8, cols].astype(F32)
            deltas = deltas + dos[inner + 8 : inner + 16, cols].astype(F32)
            new = []
            for e, h in enumerate(heads):
                q, do = qs[h * 64 : h * 64 + 64, cols], dos[h * 64 : h * 64 + 64, cols]
                s = tn(ks[e], q) + tiles[h * 5 + kind]
                s = jnp.where(same, s, MASKED)
                p = jnp.exp(s - logs[h : h + 1, :])
                ds = p * (tn(vs[e], do) - deltas[h : h + 1, :])
                to_k, to_v = state[e]
                new.append((to_k + nt(q, ds.astype(BF16)), to_v + nt(do, p.astype(BF16))))
            return tuple(new)

        start = jnp.zeros((64, BLK), F32)
        state = lax.fori_loop(low, high, body, ((start, start), (start, start)))
        for e, h in enumerate(heads):
            dk[h * 64 : h * 64 + 64, :] = state[e][0].astype(BF16)
            dv[h * 64 : h * 64 + 64, :] = state[e][1].astype(BF16)


def whole_block(shape):
    return pl.BlockSpec(shape, lambda i: (0,) * len(shape))


def col_block(rows):
    return pl.BlockSpec((rows, BLK), lambda i: (0, i))


SMEM_SPEC = pl.BlockSpec(memory_space=pltpu.SMEM)
COL_SEGS = pl.BlockSpec((BLK, 1), lambda i: (i, 0))
ROW_SEGS = pl.BlockSpec((1, 1, BLK), lambda i: (i, 0, 0))
TILES = pltpu.VMEM((HEADS * 5, BLK, BLK), F32)
LIGHT = pl.CostEstimate(flops=1, bytes_accessed=1, transcendentals=0)
ATTEND_COST = pl.CostEstimate(flops=23 * 10**9, bytes_accessed=1, transcendentals=0)
FFN_COST = pl.CostEstimate(flops=48 * 10**9, bytes_accessed=1, transcendentals=0)


def params():
    return pltpu.CompilerParams(
        dimension_semantics=("arbitrary",), vmem_limit_bytes=VMEM_CAP
    )


def attend(off, span, lohi, vec, q, seg_row, seg_col, kv):
    inner, rows = q.shape
    return pl.pallas_call(
        partial(forward_kernel, off, len(kv)),
        grid=(rows // BLK,),
        in_specs=[SMEM_SPEC, whole_block(vec.shape), col_block(inner), ROW_SEGS, whole_block(seg_col.shape)]
        + [whole_block(p.shape) for p in kv],
        out_specs=[col_block(inner), col_block(inner), col_block(8), col_block(32)],
        out_shape=[
            jax.ShapeDtypeStruct((inner, rows), BF16),
            jax.ShapeDtypeStruct((inner, rows), F32),
            jax.ShapeDtypeStruct((8, rows), F32),
            jax.ShapeDtypeStruct((32, rows), BF16),
        ],
        scratch_shapes=[TILES, pltpu.VMEM((2 * inner, span), BF16)],
        cost_estimate=ATTEND_COST,
        name="attend",
        compiler_params=params(),
    )(lohi, vec, q, seg_row, seg_col, *kv)


def attend_queries(off, span, lohi, vec, q, do, lse, delta, seg_row, seg_col, kv):
    inner, rows = q.shape
    return pl.pallas_call(
        partial(query_kernel, off, len(kv)),
        grid=(rows // BLK,),
        in_specs=[
            SMEM_SPEC,
            whole_block(vec.shape),
            col_block(inner),
            col_block(inner),
            col_block(8),
            col_block(8),
            ROW_SEGS,
            whole_block(seg_col.shape),
        ]
        + [whole_block(p.shape) for p in kv],
        out_specs=[
            col_block(inner),
            whole_block((HEADS, 8, SPAN)),
            whole_block((HEADS, 2, 8, BLK)),
        ],
        out_shape=[
            jax.ShapeDtypeStruct((inner, rows), BF16),
            jax.ShapeDtypeStruct((HEADS, 8, SPAN), F32),
            jax.ShapeDtypeStruct((HEADS, 2, 8, BLK), F32),
        ],
        scratch_shapes=[TILES, TILES, pltpu.VMEM((2 * inner, span), BF16)],
        cost_estimate=ATTEND_COST,
        name="attend_queries",
        compiler_params=params(),
    )(lohi, vec, q, do, lse, delta, seg_row, seg_col, *kv)


def attend_keys(off, span, lohi, vec, k, v, seg_row, seg_col, queries, answers):
    inner, rows = k.shape
    both = list(queries) + list(answers)
    return pl.pallas_call(
        partial(key_kernel, off, len(queries)),
        grid=(rows // BLK,),
        in_specs=[
            SMEM_SPEC,
            whole_block(vec.shape),
            col_block(inner),
            col_block(inner),
            whole_block(seg_row.shape),
            COL_SEGS,
        ]
        + [whole_block(p.shape) for p in both],
        out_specs=[col_block(inner), col_block(inner)],
        out_shape=[jax.ShapeDtypeStruct((inner, rows), BF16)] * 2,
        scratch_shapes=[
            TILES,
            pltpu.VMEM((queries[0].shape[0], span), BF16),
            pltpu.VMEM((answers[0].shape[0], span), BF16),
        ],
        cost_estimate=ATTEND_COST,
        name="attend_keys",
        compiler_params=params(),
    )(lohi, vec, k, v, seg_row, seg_col, *both)


def ffn_kernel(nm, half, count, groups, order, na, nb, ca, cb, nat, nbt, cat, cbt, *rest):
    pieces = rest[:count]
    out_a, out_b, gn_a, gn_b, *grads = rest[count : count + 4 + len(groups)]
    weights, x, ct, hid, ggr, gur, sem = rest[count + 4 + len(groups) :]
    i = pl.program_id(0)

    @pl.when(i == 0)
    def _():
        copies = []
        for piece in pieces:
            rows = piece.shape[2]
            for n in range(piece.shape[0]):
                k = len(copies) // 3
                at = pl.multiple_of(order[k], 16)
                for m in range(3):
                    copies.append(
                        pltpu.make_async_copy(
                            piece.at[n, m], weights.at[m, pl.ds(at, rows), :], sem.at[k, m]
                        )
                    )
        for copy in copies:
            copy.start()
        for copy in copies:
            copy.wait()

    @pl.when(i < half)
    def _():
        x[...] = na[...].T
        ct[...] = ca[...].T

    @pl.when((i >= half) & (i < nm))
    def _():
        x[...] = nb[...].T
        ct[...] = cb[...].T

    @pl.when(i < nm)
    def _():
        rows = pl.ds(pl.multiple_of(i * BLK, BLK), BLK)
        g = nn(x[...], weights[0])
        u = nn(x[...], weights[1])
        gh = nn(ct[...], weights[2])
        square = g * g
        t = jnp.tanh(GELU_K * g * (1.0 + GELU_A * square))
        part = 0.5 * (1.0 + t)
        gelu = g * part
        slope = part + 0.5 * g * (1.0 - t * t) * (GELU_K * (1.0 + 3.0 * GELU_A * square))
        h = (gelu * u).astype(BF16)
        gg = (gh * u * slope).astype(BF16)
        gu = (gh * gelu).astype(BF16)
        hid[rows, :] = h
        ggr[rows, :] = gg
        gur[rows, :] = gu
        out = nt(weights[2], h).astype(BF16)
        gn = (nt(weights[0], gg) + nt(weights[1], gu)).astype(BF16)

        @pl.when(i < half)
        def _():
            out_a[...] = out
            gn_a[...] = gn

        @pl.when(i >= half)
        def _():
            out_b[...] = out
            gn_b[...] = gn

    @pl.when(i >= nm)
    def _():
        t = hid.shape[0] // 2

        def product(first, second, right):
            return (nn(first[...], right[:t, :]) + nn(second[...], right[t:, :])).astype(BF16)

        lefts = ((nat, nbt, ggr), (nat, nbt, gur), (cat, cbt, hid))
        for g, members in enumerate(groups):
            for n, m in enumerate(members):
                grads[g][0, n] = product(*lefts[m])


def ffn(n_own, n_other, c_own, c_other, pieces, starts, groups):
    depth, t = n_own.shape
    cols = pieces[0].shape[3]
    half = t // BLK
    nm = 2 * half
    tile = depth // 4
    scalars = jnp.stack([jnp.asarray(v, jnp.int32) for v in starts])
    own = pl.BlockSpec((depth, BLK), lambda i, o: (0, jnp.minimum(i, half - 1)))
    other = pl.BlockSpec((depth, BLK), lambda i, o: (0, jnp.clip(i - half, 0, half - 1)))
    later = pl.BlockSpec((tile, t), lambda i, o: (jnp.maximum(i - nm, 0), 0))
    place = pl.BlockSpec(memory_space=pl.ANY)
    grads = [
        pl.BlockSpec((1, len(m), tile, cols), lambda i, o: (jnp.maximum(i - nm, 0), 0, 0, 0)) for m in groups
    ]
    return pl.pallas_call(
        partial(ffn_kernel, nm, half, len(pieces), groups),
        grid_spec=pltpu.PrefetchScalarGridSpec(
            num_scalar_prefetch=1,
            grid=(nm + 4,),
            in_specs=[own, other, own, other, later, later, later, later] + [place] * len(pieces),
            out_specs=[own, other, own, other] + grads,
            scratch_shapes=[
                pltpu.VMEM((3, depth, cols), BF16),
                pltpu.VMEM((BLK, depth), BF16),
                pltpu.VMEM((BLK, depth), BF16),
                pltpu.VMEM((2 * t, cols), BF16),
                pltpu.VMEM((2 * t, cols), BF16),
                pltpu.VMEM((2 * t, cols), BF16),
                pltpu.SemaphoreType.DMA((len(starts), 3)),
            ],
        ),
        out_shape=[jax.ShapeDtypeStruct((depth, t), BF16)] * 4
        + [jax.ShapeDtypeStruct((4, len(m), tile, cols), BF16) for m in groups],
        cost_estimate=FFN_COST,
        name="ffn",
        compiler_params=params(),
    )(scalars, n_own, n_other, c_own, c_other, n_own, n_other, c_own, c_other, *pieces)


def rms_scale(x):
    return lax.rsqrt(jnp.mean(x * x, axis=0, keepdims=True) + EPS)


def norm_back(grad, x, scale, gain):
    gain_grad = jnp.sum(grad * (x * scale), axis=1)
    weighted = grad * gain
    dots = jnp.mean(weighted * x, axis=0, keepdims=True)
    return scale * weighted - x * (scale * scale * scale * dots), gain_grad


def on_device(
    n_dp,
    n_seq,
    inputs,
    segments,
    cotangent,
    w_query,
    w_key,
    w_value,
    w_out,
    w_gate,
    w_up,
    w_down,
    gain_attn,
    gain_ffn,
    rel_table,
):
    mv = Moves(n_dp, n_seq)
    seqs, rows, depth = inputs.shape
    source = inputs.reshape(seqs * rows, depth).T.astype(F32)
    tangent = cotangent.reshape(seqs * rows, depth).T
    rw, sc = w_query.shape
    inner = sc * n_seq
    wide = 4 * sc
    seg_rows = -(-rows // wide)
    rp = -(-(rw + 2 + seg_rows) // 16) * 16

    body = jnp.concatenate([w_query, w_key, w_value, w_out.T], axis=1)
    table_row = rel_table.reshape(-1)
    pad_to = lambda v: jnp.pad(v, (0, -v.shape[0] % wide)).reshape(-1, wide)
    packed = jnp.concatenate(
        [
            body,
            pad_to(jnp.concatenate([gain_attn, gain_ffn])),
            pad_to(table_row),
            pad_to(segments.reshape(rows).astype(BF16)),
            jnp.zeros((rp - rw - 2 - seg_rows, wide), BF16),
        ],
        axis=0,
    )
    att, stages = gather_small(mv, packed)
    full = att[:, :, :rw, :].reshape(n_seq, depth, wide)
    gain_one = att[0, :, rw, :rw].reshape(depth, 1).astype(F32)
    gain_two = att[0, :, rw, rw : 2 * rw].reshape(depth, 1).astype(F32)
    table = att[0, :, rw + 1, : table_row.shape[0]].reshape(BUCKETS, HEADS)
    here = lax.dynamic_index_in_dim(att, lax.axis_index("dp"), 1, keepdims=False)
    seg_seq = here[:, rw + 2 : rw + 2 + seg_rows, :].reshape(n_seq, -1)[:, :rows].astype(jnp.int32)

    scale_one = rms_scale(source)
    normed = ((source * scale_one) * gain_one).astype(BF16)
    qkv = jnp.einsum("zdc,dt->zct", full[:, :, : 3 * sc], normed, preferred_element_type=F32)
    qkv = jnp.transpose(qkv.astype(BF16).reshape(n_seq, 3, sc, rows), (1, 0, 2, 3))
    q = qkv[0].reshape(inner, rows)
    k = qkv[1].reshape(inner, rows)
    v = qkv[2].reshape(inner, rows)

    zh = n_seq // 2
    small = small_plane(mv)
    tangent_other = mv.rotate(tangent, "c")
    cores = gather_core(mv, jnp.stack([w_gate, w_up, w_down.T]), (q, tangent_other))
    kv_halo = halo(mv, after(jnp.concatenate([k, v], 0), cores[0]))
    pieces, starts = [], []
    for j in range(zh):
        full_block = lax.all_gather(cores[j], "dp", axis_index_groups=mv.same_core())
        if small:
            pieces.append([full_block])
            starts.append([jnp.int32(2 * rw * k) for k in range(4)])
        else:
            pieces.append([jnp.moveaxis(full_block, 0, 1).reshape(1, 3, depth, -1)])
            starts.append([jnp.int32(0)])

    off = -(-MAX_DOC // BLK) * BLK
    span = 2 * off + rows
    blocks = span // BLK
    seg_own = segments.reshape(rows)
    line = jnp.pad(seg_seq.reshape(-1), (off, off), constant_values=-1)
    seg_all = lax.dynamic_slice_in_dim(line, mv.index["z"] * rows, span, 0)
    seg_row = seg_all.reshape(blocks, 1, BLK)
    seg_col = seg_all.reshape(span, 1)
    own_row = seg_own.reshape(rows // BLK, 1, BLK)
    own_col = seg_own.reshape(rows, 1)
    spots = jnp.arange(span, dtype=jnp.int32)
    firsts = seg_own[::BLK]
    lasts = seg_own[BLK - 1 :: BLK]
    low = jnp.min(jnp.where(seg_all[None] == firsts[:, None], spots[None], 1 << 20), axis=1) // BLK
    high = jnp.max(jnp.where(seg_all[None] == lasts[:, None], spots[None], -1), axis=1) // BLK + 1
    lohi = jnp.stack([low, high], 1).astype(jnp.int32)

    buckets = bucket_table()
    buckets = np.concatenate([buckets[-1:], buckets[:0:-1]])
    chosen = jnp.asarray((buckets[:, None] == np.arange(BUCKETS)[None, :]), BF16)
    vec = dot(table, chosen, ((0,), (1,)))

    attended, exact, lse, lse_parts = attend(
        off, span, lohi, vec, q, own_row, seg_col, kv_halo
    )
    q_halo = halo(mv, jnp.concatenate([q, lse_parts], 0))

    mixed = source + jnp.einsum(
        "zdc,zct->dt", full[:, :, 3 * sc :], attended.reshape(n_seq, sc, rows), preferred_element_type=F32
    )
    scale_two = rms_scale(mixed)
    normed_two = ((mixed * scale_two) * gain_two).astype(BF16)

    normed_other = mv.rotate(normed_two, "c")
    parts, sums = [], []
    for j in range(zh):
        results = ffn(
            after(normed_two, *(list(parts[-1]) + q_halo if j else ())),
            normed_other,
            tangent,
            tangent_other,
            pieces[j],
            starts[j],
            ((0, 1, 2),) if j + 1 < zh else ((0, 1), (2,)),
        )
        parts.append(results[:4])
        sums.append([ZSum(mv, j, scatter_plane(mv, grad)) for grad in results[4:]])
    out_own, out_other, gn_own, gn_other = (
        sum(four[m].astype(F32) for four in parts) for m in range(4)
    )
    gn_recv = mv.rotate(gn_other.astype(BF16), "c")
    grad_n2 = gn_own + gn_recv.astype(F32)

    grad_mixed, grad_gain_two = norm_back(grad_n2, mixed, scale_two, gain_two)
    grad_mixed = grad_mixed + tangent.astype(F32)
    grad_branch = grad_mixed.astype(BF16)
    grad_att = jnp.einsum(
        "zdc,dt->zct", full[:, :, 3 * sc :], grad_branch, preferred_element_type=F32
    )
    grad_att = grad_att.reshape(inner, rows).astype(BF16)
    delta = jnp.sum((grad_att.astype(F32) * exact).reshape(HEADS, inner // HEADS, rows), axis=1)
    delta = jnp.pad(delta, ((0, 8 - HEADS), (0, 0)))
    delta_top = lax.reduce_precision(delta, 8, 7)
    answers = jnp.concatenate([grad_att, delta_top.astype(BF16), (delta - delta_top).astype(BF16)], 0)
    do_halo = halo(mv, answers, False)

    dq, near, far = attend_queries(
        off, span, lohi, vec, q, grad_att, lse, delta, own_row, seg_col, kv_halo
    )
    out_recv = mv.rotate(after(out_other.astype(BF16), do_halo[0]), "c")
    outputs = (mixed + out_own + out_recv.astype(F32)).astype(BF16)
    swaps = [u.swap(do_halo[0]) for u in sums[0]]
    k_then = after(k, dq)
    dk, dv = attend_keys(off, span, lohi, vec, k_then, v, seg_row, own_col, q_halo, do_halo)
    if small:
        dk = after(dk, *swaps)

    sheared = jnp.roll(jnp.sum(near, axis=1), BLK, axis=1)
    grad_table = jnp.dot(sheared, chosen.astype(F32), precision=lax.Precision.HIGHEST).T
    far_sums = jnp.sum(far, axis=(2, 3))
    grad_table = grad_table.at[31].add(far_sums[:, 0]).at[15].add(far_sums[:, 1])

    split = lambda x: x.reshape(n_seq, sc, rows)
    rows_z = jnp.concatenate([split(dq), split(dk), split(dv)], axis=1)
    grad_normed = jnp.einsum(
        "zdc,zct->dt", full[:, :, : 3 * sc], rows_z, preferred_element_type=F32
    )
    grad_source, grad_gain_one = norm_back(grad_normed, source, scale_one, gain_one)
    input_grad = (grad_mixed + grad_source).astype(BF16)

    g_in = jnp.einsum("dt,zct->zdc", normed, rows_z, preferred_element_type=F32)
    g_out = jnp.einsum("dt,zct->zdc", grad_branch, split(attended), preferred_element_type=F32)
    grads = jnp.concatenate([g_in, g_out], axis=2).reshape(n_seq, n_dp, rw, wide)
    gain_rows = jnp.concatenate(
        [grad_gain_one.reshape(n_dp, rw), grad_gain_two.reshape(n_dp, rw)], axis=1
    )
    widen = lambda x: jnp.broadcast_to(
        jnp.pad(x, ((0, 0), (0, wide - x.shape[1])))[None, :, None, :], (n_seq, n_dp, 1, wide)
    )
    grads = jnp.concatenate(
        [
            grads,
            widen(gain_rows),
            widen(grad_table.reshape(n_dp, -1)),
            jnp.zeros((n_seq, n_dp, rp - rw - 2, wide), F32),
        ],
        axis=2,
    ).astype(BF16)
    if small:
        (first,), (wide, thin) = sums
        grads = after(grads, first.inwards())
        wide.swap(grads)
    else:
        for units in sums[1:]:
            for u in units:
                u.swap(None)

    def before_plane(x):
        return [first.across(), thin.x] if small else []

    def midway(x):
        return [thin.swap(x), wide.inwards(), first.home()] if small else []

    def before_z(x):
        return [wide.across(), thin.inwards()] if small else []

    own = scatter_small(mv, grads, before_plane, midway, before_z)
    if small:
        wide.home()
        thin.across()
        thin.home()
    own_ffn = z_totals(mv, sums)

    return (
        outputs.T.reshape(seqs, rows, depth),
        input_grad.T.reshape(seqs, rows, depth),
        own[:rw, :sc],
        own[:rw, sc : 2 * sc],
        own[:rw, 2 * sc : 3 * sc],
        own[:rw, 3 * sc :].T,
        own_ffn[0],
        own_ffn[1],
        own_ffn[2].T,
        own[rw, :rw],
        own[rw, rw : 2 * rw],
        own[rw + 1, : table_row.shape[0]].reshape(rel_table.shape),
    )


def solution(mesh):
    row, col = P("dp", "seq"), P("seq", "dp")
    tokens = P("dp", "seq", None)
    return jax.shard_map(
        partial(on_device, mesh.shape["dp"], mesh.shape["seq"]),
        mesh=mesh,
        in_specs=(tokens, row, tokens, row, row, row, col, row, row, col, P("dp"), P("dp"), P("dp", None)),
        out_specs=(tokens, tokens, row, row, row, col, row, row, col, P("dp"), P("dp"), P("dp", None)),
        check_vma=False,
    )
```

```python
import math
from functools import partial

import jax
import jax.numpy as jnp
import numpy as np
from jax import lax
from jax.experimental import pallas as pl
from jax.experimental.pallas import tpu as pltpu
from jax.sharding import PartitionSpec as P

HEADS = 6
BUCKETS = 32
MAX_DOC = 800
BLK = 256
SPAN = 1024
EPS = 1e-06
MASKED = -1e30
F32 = jnp.float32
BF16 = jnp.bfloat16
VMEM_CAP = 58 * 1024 * 1024
LANES = 128
GELU_K = math.sqrt(2.0 / math.pi)
GELU_A = 0.044715


def bucket_table():
    relative = np.arange(SPAN) - SPAN // 2
    distance = np.abs(relative)
    steps = np.array([12, 16, 23, 32, 46, 64, 91])
    levels = (distance[:, None] >= steps[None, :]).sum(axis=1)
    inside = np.where(distance < 8, distance, 8 + levels)
    return (inside + 16 * (relative > 0)).astype(np.int32)


class Moves:
    def __init__(self, n_dp, n_seq):
        self.n_dp, self.n_seq = n_dp, n_seq
        plane = n_dp // 2
        side = int(round(math.sqrt(plane)))
        self.size = {"a": plane // side, "b": side, "c": 2, "z": n_seq}
        dp = lax.axis_index("dp")
        self.last = {}
        self.index = {
            "a": dp // (2 * side),
            "b": (dp // 2) % side,
            "c": dp % 2,
            "z": lax.axis_index("seq"),
        }

    def rotate(self, x, axis):
        n = self.size[axis]
        if axis == "z":
            return lax.ppermute(x, "seq", [(i, (i + 1) % n) for i in range(n)])
        pairs = []
        side = self.size["b"]
        for i in range(self.n_dp):
            a, b, c = i // (2 * side), (i // 2) % side, i % 2
            if axis == "a":
                a = (a + 1) % n
            elif axis == "b":
                b = (b + 1) % n
            else:
                c = 1 - c
            pairs.append((i, (a * side + b) * 2 + c))
        return lax.ppermute(x, "dp", pairs)

    def zperm(self, x, pairs):
        return lax.ppermute(x, "seq", pairs)

    def same_core(self):
        return [list(range(c, self.n_dp, 2)) for c in range(2)]

    def ring(self, x, waits=()):
        parts = []
        for step in range(self.n_seq - 1):
            x = self.rotate(after(x, *waits[step]) if step < len(waits) else x, "z")
            parts.append(x)
        return parts

    def gather(self, x, axis, at=0):
        n, i = self.size[axis], self.index[axis]
        if n == 2:
            other = self.rotate(x, axis)
            return ordered(i == 0, x, other, at)
        parts = [x]
        for _ in range(n - 1):
            parts.append(self.rotate(parts[-1], axis))
        turned = jnp.stack(parts[::-1] + parts[::-1], 0)
        full = lax.dynamic_slice_in_dim(turned, n - 1 - i, n, 0)
        return jnp.moveaxis(full, 0, at)

    def scatter(self, x, axis, at=0, out=BF16):
        n, i = self.size[axis], self.index[axis]
        take = lambda k: lax.dynamic_index_in_dim(x, k, at, keepdims=False)
        if n == 2:
            other = self.rotate(take(1 - i), axis)
            return add(take(i), other, out)
        acc = take((i + n - 1) % n)
        for step in range(n - 1):
            got = self.rotate(acc, axis)
            last = step == n - 2
            acc = add(take((i + 2 * n - 2 - step) % n), got, out if last else BF16)
        return acc


def after(x, *others):
    others = [o for o in others if o is not None]
    return lax.optimization_barrier((x, *others))[0] if others else x


def add(x, y, out):
    return (x.astype(F32) + y.astype(F32)).astype(out)


def ordered(first, x, y, at):
    return jnp.stack([jnp.where(first, x, y), jnp.where(first, y, x)], at)


def z_gather(mv, w, waits=()):
    z, n = mv.index["z"], mv.n_seq
    blocks = [w] + mv.ring(w, waits)
    turned = jnp.stack(blocks[::-1] + blocks[::-1], 0)
    return lax.dynamic_slice_in_dim(turned, n - 1 - z, n, 0)


def small_plane(mv):
    return mv.size["a"] == 2 and mv.size["b"] == 2 and mv.n_seq == 4


def gather_core(mv, w, ready):
    k, rows, cols = w.shape
    c = mv.index["c"]
    full = lax.all_gather(w, "seq")
    zh = mv.n_seq // 2
    keep = lax.dynamic_slice_in_dim(full, c * zh, zh, 0)
    send = lax.dynamic_slice_in_dim(full, (1 - c) * zh, zh, 0)
    recv = mv.rotate(after(send, *ready), "c")
    block = ordered(c == 0, keep, recv, 2)
    return [block[j].reshape(k, 2 * rows, cols) for j in range(zh)]


def scatter_plane(mv, grad):
    quarter, k, rows, cols = grad.shape
    chips = mv.n_dp // 2
    x = grad
    if chips != quarter:
        x = jnp.moveaxis(grad, 1, 0).reshape(k, chips, quarter * rows // chips, cols)
        x = jnp.moveaxis(x, 0, 1)
    x = lax.psum_scatter(x, "dp", scatter_dimension=0, axis_index_groups=mv.same_core())
    x = x.reshape(k, 2, x.shape[1] // 2, cols)
    return x


def swap_cores(mv, x):
    c = mv.index["c"]
    take = lambda i: lax.dynamic_index_in_dim(x, i, 1, keepdims=False)
    return take(c), mv.rotate(take(1 - c), "c")


class ZSum:
    def __init__(self, mv, j, x):
        self.mv, self.j, self.x = mv, j, x

    def swap(self, wait):
        c = self.mv.index["c"]
        x = after(self.x, wait)
        take = lambda i: lax.dynamic_index_in_dim(x, i, 1, keepdims=False)
        mine, other = take(c), self.mv.rotate(take(1 - c), "c")
        here = (self.mv.index["z"] // 2) == c
        self.pair = mine, other
        self.near, self.far = jnp.where(here, mine, other), jnp.where(here, other, mine)
        return other

    def inwards(self, wait=None):
        got = self.mv.zperm(after(self.far, wait), [(0, 1), (3, 2)])
        self.far = add(self.far, got, BF16)
        return got

    def across(self, wait=None):
        got = self.mv.zperm(after(self.far, wait), [(1, 2), (2, 1)])
        self.near = add(self.near, got, BF16)
        return got

    def home(self, wait=None):
        j = self.j
        got = self.mv.zperm(after(self.near, wait), [(1 - j, j), (3 - j, 2 + j)])
        self.total = add(self.near, got, F32)
        return got


def z_totals(mv, sums):
    z, c = mv.index["z"], mv.index["c"]
    join = lambda parts: jnp.concatenate(parts, 0)
    if mv.n_seq == 4:
        first, second = (join([u.total for u in units]) for units in sums)
        return jnp.where(z % 2 == 0, first, second)
    full = jnp.stack(
        [ordered(c == 0, *(join([u.pair[i] for u in units]) for i in range(2)), 0) for units in sums], 1
    )
    return mv.scatter(full.reshape((mv.n_seq,) + full.shape[2:]), "z", 0, F32)


def gather_small(mv, w):
    full = z_gather(mv, w)
    half = mv.n_seq // 2
    lo_one = mv.gather(full[:half], "b", 1)
    hi_one = mv.gather(full[half:], "a", 1)
    lo = mv.gather(lo_one, "a", 1)
    hi = mv.gather(hi_one, "b", 2)
    both = jnp.concatenate([lo, hi], 0)
    both = mv.gather(both, "c", 3)
    return both.reshape((mv.n_seq, mv.n_dp) + w.shape), (full, (lo_one, hi_one), (lo, hi))


def scatter_small(mv, send, keep):
    both = add(keep, mv.rotate(send, "c"), BF16)
    x = lax.psum_scatter(both, "dp", scatter_dimension=0, axis_index_groups=mv.same_core())
    return lax.psum_scatter(x, "seq", scatter_dimension=0).astype(F32), both


def reach_of(rows, n_seq):
    need, parts = MAX_DOC - 1, []
    while need > 0 and len(parts) + 1 < n_seq:
        parts.append(min(rows, -(-need // LANES) * LANES))
        need -= rows
    return parts


def halo(mv, x, chained=True):
    rows, n = x.shape[1], mv.n_seq
    left, right = [], []
    own = x
    for hop, cols in enumerate(reach_of(rows, n)):
        step = hop + 1
        if chained and hop > 0:
            x = after(x, left[0], right[-1])
        left.insert(0, mv.zperm(x[:, rows - cols :], [(i, i + step) for i in range(n - step)]))
        right.append(mv.zperm(x[:, :cols], [(i + step, i) for i in range(n - step)]))
    return left + [own] + right


def dot(x, y, dims):
    return lax.dot_general(x, y, (dims, ((), ())), preferred_element_type=F32)


def nt(x, y):
    return dot(x, y, ((1,), (1,)))


def nn(x, y):
    return dot(x, y, ((1,), (0,)))


def tn(x, y):
    return dot(x, y, ((0,), (0,)))


def make_tiles(vec_ref, tiles):
    for h in range(HEADS):
        line = vec_ref[h : h + 1, :]
        wide = jnp.broadcast_to(line, (BLK, SPAN))
        rolled = pltpu.roll(wide, 0, 1, stride=1, stride_axis=0)
        tiles[h * 5] = jnp.broadcast_to(line[:, :1], (BLK, BLK))
        tiles[h * 5 + 4] = jnp.broadcast_to(line[:, SPAN - 1 :], (BLK, BLK))
        for d in (-1, 0, 1):
            at = SPAN // 2 + BLK * d
            tiles[h * 5 + 2 + d] = rolled[:, at : at + BLK]


def class_of(query_block, key_block):
    return jnp.clip(query_block - key_block, -2, 2) + 2


def lay_out(off, pieces, whole):
    middle = len(pieces) // 2
    at = off - sum(p.shape[1] for p in pieces[:middle])
    if at > 0:
        whole[:, :at] = jnp.zeros((whole.shape[0], at), whole.dtype)
    for p in pieces:
        whole[:, at : at + p.shape[1]] = p[...]
        at += p.shape[1]
    if at < whole.shape[1]:
        whole[:, at:] = jnp.zeros((whole.shape[0], whole.shape[1] - at), whole.dtype)


def block_at(k):
    return pl.ds(pl.multiple_of(k * BLK, BLK), BLK)


def forward_kernel(off, count, lohi, vec, q_ref, segq, segk, *rest):
    pieces = rest[:count]
    out, exact, lse, split, tiles, kv = rest[count:]
    i = pl.program_id(0)

    @pl.when(i == 0)
    def _():
        make_tiles(vec, tiles)
        lay_out(off, pieces, kv)

    own = off // BLK + i
    inner = HEADS * 64
    low, high = lohi[i, 0], lohi[i, 1]
    seg_row = segq[0]
    split[...] = jnp.zeros_like(split)
    lse[...] = jnp.zeros_like(lse)
    for pair in range(HEADS // 2):
        heads = (2 * pair, 2 * pair + 1)
        qs = [q_ref[h * 64 : h * 64 + 64, :] for h in heads]

        def body(kb, state):
            cols = block_at(kb)
            same = segk[cols, :] == seg_row
            kind = class_of(own, kb)
            new = []
            for e, h in enumerate(heads):
                peak, total, acc = state[e]
                s = tn(kv[h * 64 : h * 64 + 64, cols], qs[e]) + tiles[h * 5 + kind]
                s = jnp.where(same, s, MASKED)
                top = jnp.maximum(peak, jnp.max(s, axis=0, keepdims=True))
                fade = jnp.exp(peak - top)
                p = jnp.exp(s - top)
                total = total * fade + jnp.sum(p, axis=0, keepdims=True)
                acc = acc * fade + nn(kv[inner + h * 64 : inner + h * 64 + 64, cols], p.astype(BF16))
                new.append((top, total, acc))
            return tuple(new)

        start = (
            jnp.full((1, BLK), MASKED, F32),
            jnp.zeros((1, BLK), F32),
            jnp.zeros((64, BLK), F32),
        )
        state = lax.fori_loop(low, high, body, (start, start))
        for e, h in enumerate(heads):
            peak, total, acc = state[e]
            done = acc / total
            out[h * 64 : h * 64 + 64, :] = done.astype(BF16)
            exact[h * 64 : h * 64 + 64, :] = done
            log = peak + jnp.log(total)
            lse[h : h + 1, :] = log
            for part in range(3):
                piece = log.astype(BF16)
                split[part * 8 + h : part * 8 + h + 1, :] = piece
                log = log - piece.astype(F32)


def query_kernel(off, count, lohi, vec, q_ref, do_ref, lse, delta, segq, segk, *rest):
    pieces = rest[:count]
    dq, near, far, tiles, sums, kv = rest[count:]
    i = pl.program_id(0)

    @pl.when(i == 0)
    def _():
        make_tiles(vec, tiles)
        lay_out(off, pieces, kv)
        sums[...] = jnp.zeros_like(sums)

    own = off // BLK + i
    inner = HEADS * 64
    low, high = lohi[i, 0], lohi[i, 1]
    seg_row = segq[0]
    for pair in range(HEADS // 2):
        heads = (2 * pair, 2 * pair + 1)
        qs = [q_ref[h * 64 : h * 64 + 64, :] for h in heads]
        dos = [do_ref[h * 64 : h * 64 + 64, :] for h in heads]

        def body(kb, state):
            cols = block_at(kb)
            same = segk[cols, :] == seg_row
            kind = class_of(own, kb)
            new = []
            for e, h in enumerate(heads):
                keys = kv[h * 64 : h * 64 + 64, cols]
                s = tn(keys, qs[e]) + tiles[h * 5 + kind]
                s = jnp.where(same, s, MASKED)
                p = jnp.exp(s - lse[h : h + 1, :])
                dp = tn(kv[inner + h * 64 : inner + h * 64 + 64, cols], dos[e])
                ds = p * (dp - delta[h : h + 1, :])
                at = h * 5 + kind
                sums[at] = sums[at] + ds
                new.append(state[e] + nn(keys, ds.astype(BF16)))
            return tuple(new)

        start = jnp.zeros((64, BLK), F32)
        state = lax.fori_loop(low, high, body, (start, start))
        for e, h in enumerate(heads):
            dq[h * 64 : h * 64 + 64, :] = state[e].astype(BF16)

    @pl.when(i == pl.num_programs(0) - 1)
    def _():
        for h in range(HEADS):
            zero = jnp.zeros((BLK, BLK), F32)
            x = jnp.concatenate([sums[h * 5 + 1], sums[h * 5 + 2], sums[h * 5 + 3], zero], axis=1)
            n = BLK // 2
            while n >= 8:
                x = x[:n] + pltpu.roll(x[n:], SPAN - n, 1)
                n //= 2
            row = lax.broadcasted_iota(jnp.int32, x.shape, 0)
            for n in (4, 2, 1):
                x = jnp.where((row & n) != 0, pltpu.roll(x, SPAN - n, 1), x)
            near[h] = x
            far[h, 0] = jnp.sum(sums[h * 5].reshape(BLK // 8, 8, BLK), axis=0)
            far[h, 1] = jnp.sum(sums[h * 5 + 4].reshape(BLK // 8, 8, BLK), axis=0)


def key_kernel(off, count, lohi, vec, k_ref, v_ref, segq, segk, *rest):
    queries, answers = rest[:count], rest[count : 2 * count]
    dk, dv, tiles, qs, dos = rest[2 * count :]
    i = pl.program_id(0)

    @pl.when(i == 0)
    def _():
        make_tiles(vec, tiles)
        lay_out(off, queries, qs)
        lay_out(off, answers, dos)

    own = off // BLK + i
    inner = HEADS * 64
    low, high = lohi[i, 0], lohi[i, 1]
    seg_col = segk[...]
    for pair in range(HEADS // 2):
        heads = (2 * pair, 2 * pair + 1)
        ks = [k_ref[h * 64 : h * 64 + 64, :] for h in heads]
        vs = [v_ref[h * 64 : h * 64 + 64, :] for h in heads]

        def body(qb, state):
            cols = block_at(qb)
            same = seg_col == segq[qb]
            kind = class_of(qb, own)
            logs = qs[inner : inner + 8, cols].astype(F32)
            logs = logs + qs[inner + 8 : inner + 16, cols].astype(F32)
            logs = logs + qs[inner + 16 : inner + 24, cols].astype(F32)
            deltas = dos[inner : inner + 8, cols].astype(F32)
            deltas = deltas + dos[inner + 8 : inner + 16, cols].astype(F32)
            new = []
            for e, h in enumerate(heads):
                q, do = qs[h * 64 : h * 64 + 64, cols], dos[h * 64 : h * 64 + 64, cols]
                s = tn(ks[e], q) + tiles[h * 5 + kind]
                s = jnp.where(same, s, MASKED)
                p = jnp.exp(s - logs[h : h + 1, :])
                ds = p * (tn(vs[e], do) - deltas[h : h + 1, :])
                to_k, to_v = state[e]
                new.append((to_k + nt(q, ds.astype(BF16)), to_v + nt(do, p.astype(BF16))))
            return tuple(new)

        start = jnp.zeros((64, BLK), F32)
        state = lax.fori_loop(low, high, body, ((start, start), (start, start)))
        for e, h in enumerate(heads):
            dk[h * 64 : h * 64 + 64, :] = state[e][0].astype(BF16)
            dv[h * 64 : h * 64 + 64, :] = state[e][1].astype(BF16)


def whole_block(shape):
    return pl.BlockSpec(shape, lambda i: (0,) * len(shape))


def col_block(rows):
    return pl.BlockSpec((rows, BLK), lambda i: (0, i))


SMEM_SPEC = pl.BlockSpec(memory_space=pltpu.SMEM)
COL_SEGS = pl.BlockSpec((BLK, 1), lambda i: (i, 0))
ROW_SEGS = pl.BlockSpec((1, 1, BLK), lambda i: (i, 0, 0))
TILES = pltpu.VMEM((HEADS * 5, BLK, BLK), F32)
LIGHT = pl.CostEstimate(flops=1, bytes_accessed=1, transcendentals=0)
ATTEND_COST = pl.CostEstimate(flops=23 * 10**9, bytes_accessed=1, transcendentals=0)
FFN_COST = pl.CostEstimate(flops=48 * 10**9, bytes_accessed=1, transcendentals=0)


def params():
    return pltpu.CompilerParams(
        dimension_semantics=("arbitrary",), vmem_limit_bytes=VMEM_CAP
    )


def attend(off, span, lohi, vec, q, seg_row, seg_col, kv):
    inner, rows = q.shape
    return pl.pallas_call(
        partial(forward_kernel, off, len(kv)),
        grid=(rows // BLK,),
        in_specs=[SMEM_SPEC, whole_block(vec.shape), col_block(inner), ROW_SEGS, whole_block(seg_col.shape)]
        + [whole_block(p.shape) for p in kv],
        out_specs=[col_block(inner), col_block(inner), col_block(8), col_block(32)],
        out_shape=[
            jax.ShapeDtypeStruct((inner, rows), BF16),
            jax.ShapeDtypeStruct((inner, rows), F32),
            jax.ShapeDtypeStruct((8, rows), F32),
            jax.ShapeDtypeStruct((32, rows), BF16),
        ],
        scratch_shapes=[TILES, pltpu.VMEM((2 * inner, span), BF16)],
        cost_estimate=ATTEND_COST,
        name="attend",
        compiler_params=params(),
    )(lohi, vec, q, seg_row, seg_col, *kv)


def attend_queries(off, span, lohi, vec, q, do, lse, delta, seg_row, seg_col, kv):
    inner, rows = q.shape
    return pl.pallas_call(
        partial(query_kernel, off, len(kv)),
        grid=(rows // BLK,),
        in_specs=[
            SMEM_SPEC,
            whole_block(vec.shape),
            col_block(inner),
            col_block(inner),
            col_block(8),
            col_block(8),
            ROW_SEGS,
            whole_block(seg_col.shape),
        ]
        + [whole_block(p.shape) for p in kv],
        out_specs=[
            col_block(inner),
            whole_block((HEADS, 8, SPAN)),
            whole_block((HEADS, 2, 8, BLK)),
        ],
        out_shape=[
            jax.ShapeDtypeStruct((inner, rows), BF16),
            jax.ShapeDtypeStruct((HEADS, 8, SPAN), F32),
            jax.ShapeDtypeStruct((HEADS, 2, 8, BLK), F32),
        ],
        scratch_shapes=[TILES, TILES, pltpu.VMEM((2 * inner, span), BF16)],
        cost_estimate=ATTEND_COST,
        name="attend_queries",
        compiler_params=params(),
    )(lohi, vec, q, do, lse, delta, seg_row, seg_col, *kv)


def attend_keys(off, span, lohi, vec, k, v, seg_row, seg_col, queries, answers):
    inner, rows = k.shape
    both = list(queries) + list(answers)
    return pl.pallas_call(
        partial(key_kernel, off, len(queries)),
        grid=(rows // BLK,),
        in_specs=[
            SMEM_SPEC,
            whole_block(vec.shape),
            col_block(inner),
            col_block(inner),
            whole_block(seg_row.shape),
            COL_SEGS,
        ]
        + [whole_block(p.shape) for p in both],
        out_specs=[col_block(inner), col_block(inner)],
        out_shape=[jax.ShapeDtypeStruct((inner, rows), BF16)] * 2,
        scratch_shapes=[
            TILES,
            pltpu.VMEM((queries[0].shape[0], span), BF16),
            pltpu.VMEM((answers[0].shape[0], span), BF16),
        ],
        cost_estimate=ATTEND_COST,
        name="attend_keys",
        compiler_params=params(),
    )(lohi, vec, k, v, seg_row, seg_col, *both)


def ffn_kernel(count, groups, order, na, nb, ca, cb, *rest):
    pieces = rest[:count]
    outs, grads = rest[count : count + 4], rest[count + 4 : count + 4 + len(groups)]
    weights, x, ct, hid, ggr, gur, sem = rest[count + 4 + len(groups) :]
    i = pl.program_id(0)
    t = na.shape[1]

    @pl.when(i == 0)
    def _():
        copies = []
        for piece in pieces:
            rows = piece.shape[2]
            for n in range(piece.shape[0]):
                k = len(copies) // 3
                at = pl.multiple_of(order[k], 16)
                for m in range(3):
                    copies.append(
                        pltpu.make_async_copy(
                            piece.at[n, m], weights.at[m, pl.ds(at, rows), :], sem.at[k, m]
                        )
                    )
        for copy in copies:
            copy.start()
        x[...] = na[...].T
        ct[...] = ca[...].T
        for copy in copies:
            copy.wait()

    @pl.when(i == 1)
    def _():
        x[...] = nb[...].T
        ct[...] = cb[...].T

    @pl.when(i < 2)
    def _():
        rows = pl.ds(pl.multiple_of(i * t, t), t)
        g = nn(x[...], weights[0])
        square = g * g
        th = jnp.tanh(GELU_K * g * (1.0 + GELU_A * square))
        part = 0.5 * (1.0 + th)
        gelu = g * part
        slope = part + 0.5 * g * (1.0 - th * th) * (GELU_K * (1.0 + 3.0 * GELU_A * square))
        u = nn(x[...], weights[1])
        h = (gelu * u).astype(BF16)
        gh = nn(ct[...], weights[2])
        gg = (gh * u * slope).astype(BF16)
        gu = (gh * gelu).astype(BF16)
        hid[rows, :] = h
        ggr[rows, :] = gg
        gur[rows, :] = gu
        out = nt(weights[2], h).astype(BF16)
        gn = (nt(weights[0], gg) + nt(weights[1], gu)).astype(BF16)

        @pl.when(i == 0)
        def _():
            outs[0][...] = out
            outs[2][...] = gn

        @pl.when(i == 1)
        def _():
            outs[1][...] = out
            outs[3][...] = gn

    @pl.when(i >= 2)
    def _():
        blocks, tile = grads[0].shape[0], grads[0].shape[2]
        size = blocks * tile
        rows = pl.ds(pl.multiple_of((i - 2) * size, 16), size)

        def product(first, second, right):
            return (nn(first[rows, :], right[:t, :]) + nn(second[rows, :], right[t:, :])).astype(BF16)

        lefts = ((na, nb, ggr), (na, nb, gur), (ca, cb, hid))
        for g, members in enumerate(groups):
            for n, m in enumerate(members):
                value = product(*lefts[m])
                for b in range(blocks):
                    grads[g][b, n] = value[b * tile : (b + 1) * tile]


def ffn(n_own, n_other, c_own, c_other, pieces, starts, groups):
    depth, t = n_own.shape
    cols = pieces[0].shape[3]
    tile = depth // 4
    scalars = jnp.stack([jnp.asarray(v, jnp.int32) for v in starts])
    whole = pl.BlockSpec((depth, t), lambda i, o: (0, 0), pipeline_mode=pl.Buffered(1))
    result = pl.BlockSpec((depth, t), lambda i, o: (0, 0))
    place = pl.BlockSpec(memory_space=pl.ANY)
    grads = [
        pl.BlockSpec((2, len(m), tile, cols), lambda i, o: (jnp.maximum(i - 2, 0), 0, 0, 0)) for m in groups
    ]
    return pl.pallas_call(
        partial(ffn_kernel, len(pieces), groups),
        grid_spec=pltpu.PrefetchScalarGridSpec(
            num_scalar_prefetch=1,
            grid=(4,),
            in_specs=[whole] * 4 + [place] * len(pieces),
            out_specs=[result] * 4 + grads,
            scratch_shapes=[
                pltpu.VMEM((3, depth, cols), BF16),
                pltpu.VMEM((t, depth), BF16),
                pltpu.VMEM((t, depth), BF16),
                pltpu.VMEM((2 * t, cols), BF16),
                pltpu.VMEM((2 * t, cols), BF16),
                pltpu.VMEM((2 * t, cols), BF16),
                pltpu.SemaphoreType.DMA((len(starts), 3)),
            ],
        ),
        out_shape=[jax.ShapeDtypeStruct((depth, t), BF16)] * 4
        + [jax.ShapeDtypeStruct((4, len(m), tile, cols), BF16) for m in groups],
        cost_estimate=FFN_COST,
        name="ffn",
        compiler_params=params(),
    )(scalars, n_own, n_other, c_own, c_other, *pieces)


def projection_kernel(rows, core, normed, branch, dq, dk, dv, att, extra, send, keep, left, right, value):
    t, cols = normed.shape[1], dq.shape[0]

    @pl.when(pl.program_id(0) == 0)
    def _():
        left[:, :t] = normed[...]
        left[:, t:] = branch[...]
        right[...] = jnp.zeros_like(right)

    for n, part in enumerate((dq, dk, dv)):
        right[n * cols : (n + 1) * cols, :t] = part[...]
    right[3 * cols :, t:] = att[...]
    value[...] = nt(left[...], right[...])
    for p in range(send.shape[0]):
        for ref, c in ((keep, core[0]), (send, 1 - core[0])):
            r = 2 * p + c
            block = value[pl.ds(pl.multiple_of(r * rows, 8), rows), :]
            ref[p, 0] = jnp.concatenate([block, extra[r]], axis=0).astype(BF16)


def project(core, normed, branch, dq, dk, dv, att, extra, n_seq):
    depth, t = normed.shape
    cols = dq.shape[0] // n_seq
    n_dp, more, wide = extra.shape
    rows = depth // n_dp
    whole = pl.BlockSpec((depth, t), lambda z: (0, 0))
    part = pl.BlockSpec((cols, t), lambda z: (z, 0))
    shape = (n_dp // 2, n_seq, rows + more, wide)
    result = pl.BlockSpec((n_dp // 2, 1) + shape[2:], lambda z: (0, z, 0, 0))
    return pl.pallas_call(
        partial(projection_kernel, rows),
        grid=(n_seq,),
        in_specs=[
            SMEM_SPEC,
            whole,
            whole,
            part,
            part,
            part,
            part,
            pl.BlockSpec(extra.shape, lambda z: (0, 0, 0)),
        ],
        out_specs=[result, result],
        out_shape=[jax.ShapeDtypeStruct(shape, BF16)] * 2,
        scratch_shapes=[
            pltpu.VMEM((depth, 2 * t), BF16),
            pltpu.VMEM((wide, 2 * t), BF16),
            pltpu.VMEM((depth, wide), F32),
        ],
        cost_estimate=pl.CostEstimate(flops=10**10, bytes_accessed=1, transcendentals=0),
        name="project",
        compiler_params=params(),
    )(core, normed, branch, dq, dk, dv, att, extra)


def rms_scale(x):
    return lax.rsqrt(jnp.mean(x * x, axis=0, keepdims=True) + EPS)


def norm_back(grad, x, scale, gain):
    gain_grad = jnp.sum(grad * (x * scale), axis=1)
    weighted = grad * gain
    dots = jnp.mean(weighted * x, axis=0, keepdims=True)
    return scale * weighted - x * (scale * scale * scale * dots), gain_grad


def on_device(
    n_dp,
    n_seq,
    inputs,
    segments,
    cotangent,
    w_query,
    w_key,
    w_value,
    w_out,
    w_gate,
    w_up,
    w_down,
    gain_attn,
    gain_ffn,
    rel_table,
):
    mv = Moves(n_dp, n_seq)
    seqs, rows, depth = inputs.shape
    source = inputs.reshape(seqs * rows, depth).T.astype(F32)
    tangent = cotangent.reshape(seqs * rows, depth).T
    rw, sc = w_query.shape
    inner = sc * n_seq
    wide_cols = 4 * sc
    seg_rows = -(-rows // wide_cols)
    rp = -(-(rw + 2 + seg_rows) // 16) * 16

    body = jnp.concatenate([w_query, w_key, w_value, w_out.T], axis=1)
    table_row = rel_table.reshape(-1)
    pad_to = lambda v: jnp.pad(v, (0, -v.shape[0] % wide_cols)).reshape(-1, wide_cols)
    packed = jnp.concatenate(
        [
            body,
            pad_to(jnp.concatenate([gain_attn, gain_ffn])),
            pad_to(table_row),
            pad_to(segments.reshape(rows).astype(BF16)),
            jnp.zeros((rp - rw - 2 - seg_rows, wide_cols), BF16),
        ],
        axis=0,
    )
    att, stages = gather_small(mv, packed)
    full = att[:, :, :rw, :].reshape(n_seq, depth, wide_cols)
    gain_one = att[0, :, rw, :rw].reshape(depth, 1).astype(F32)
    gain_two = att[0, :, rw, rw : 2 * rw].reshape(depth, 1).astype(F32)
    table = att[0, :, rw + 1, : table_row.shape[0]].reshape(BUCKETS, HEADS)
    here = lax.dynamic_index_in_dim(att, lax.axis_index("dp"), 1, keepdims=False)
    seg_seq = here[:, rw + 2 : rw + 2 + seg_rows, :].reshape(n_seq, -1)[:, :rows].astype(jnp.int32)

    scale_one = rms_scale(source)
    normed = ((source * scale_one) * gain_one).astype(BF16)
    qkv = jnp.einsum("zdc,dt->zct", full[:, :, : 3 * sc], normed, preferred_element_type=F32)
    qkv = jnp.transpose(qkv.astype(BF16).reshape(n_seq, 3, sc, rows), (1, 0, 2, 3))
    q = qkv[0].reshape(inner, rows)
    k = qkv[1].reshape(inner, rows)
    v = qkv[2].reshape(inner, rows)

    zh = n_seq // 2
    small = small_plane(mv)
    tangent_other = mv.rotate(tangent, "c")
    cores = gather_core(mv, jnp.stack([w_gate, w_up, w_down.T]), (q, tangent_other))
    kv_halo = halo(mv, after(jnp.concatenate([k, v], 0), cores[0]))
    pieces, starts = [], []
    for j in range(zh):
        full_block = lax.all_gather(cores[j], "dp", axis_index_groups=mv.same_core())
        if small:
            pieces.append([full_block])
            starts.append([jnp.int32(2 * rw * k) for k in range(4)])
        else:
            pieces.append([jnp.moveaxis(full_block, 0, 1).reshape(1, 3, depth, -1)])
            starts.append([jnp.int32(0)])

    off = -(-MAX_DOC // BLK) * BLK
    span = 2 * off + rows
    blocks = span // BLK
    seg_own = segments.reshape(rows)
    line = jnp.pad(seg_seq.reshape(-1), (off, off), constant_values=-1)
    seg_all = lax.dynamic_slice_in_dim(line, mv.index["z"] * rows, span, 0)
    seg_row = seg_all.reshape(blocks, 1, BLK)
    seg_col = seg_all.reshape(span, 1)
    own_row = seg_own.reshape(rows // BLK, 1, BLK)
    own_col = seg_own.reshape(rows, 1)
    spots = jnp.arange(span, dtype=jnp.int32)
    firsts = seg_own[::BLK]
    lasts = seg_own[BLK - 1 :: BLK]
    low = jnp.min(jnp.where(seg_all[None] == firsts[:, None], spots[None], 1 << 20), axis=1) // BLK
    high = jnp.max(jnp.where(seg_all[None] == lasts[:, None], spots[None], -1), axis=1) // BLK + 1
    lohi = jnp.stack([low, high], 1).astype(jnp.int32)

    buckets = bucket_table()
    buckets = np.concatenate([buckets[-1:], buckets[:0:-1]])
    chosen = jnp.asarray((buckets[:, None] == np.arange(BUCKETS)[None, :]), BF16)
    vec = dot(table, chosen, ((0,), (1,)))

    attended, exact, lse, lse_parts = attend(
        off, span, lohi, vec, q, own_row, seg_col, kv_halo
    )
    q_halo = halo(mv, jnp.concatenate([q, lse_parts], 0))

    mixed = source + jnp.einsum(
        "zdc,zct->dt", full[:, :, 3 * sc :], attended.reshape(n_seq, sc, rows), preferred_element_type=F32
    )
    scale_two = rms_scale(mixed)
    normed_two = ((mixed * scale_two) * gain_two).astype(BF16)

    normed_other = mv.rotate(normed_two, "c")
    parts, sums = [], []
    for j in range(zh):
        results = ffn(
            after(normed_two, *(list(parts[-1]) + q_halo if j else ())),
            normed_other,
            tangent,
            tangent_other,
            pieces[j],
            starts[j],
            ((0, 1, 2),) if j + 1 < zh else ((0, 1), (2,)),
        )
        parts.append(results[:4])
        sums.append([ZSum(mv, j, scatter_plane(mv, grad)) for grad in results[4:]])
    out_own, out_other, gn_own, gn_other = (
        sum(four[m].astype(F32) for four in parts) for m in range(4)
    )
    gn_recv = mv.rotate(gn_other.astype(BF16), "c")
    grad_n2 = gn_own + gn_recv.astype(F32)

    grad_mixed, grad_gain_two = norm_back(grad_n2, mixed, scale_two, gain_two)
    grad_mixed = grad_mixed + tangent.astype(F32)
    grad_branch = grad_mixed.astype(BF16)
    grad_att = jnp.einsum(
        "zdc,dt->zct", full[:, :, 3 * sc :], grad_branch, preferred_element_type=F32
    )
    grad_att = grad_att.reshape(inner, rows).astype(BF16)
    delta = jnp.sum((grad_att.astype(F32) * exact).reshape(HEADS, inner // HEADS, rows), axis=1)
    delta = jnp.pad(delta, ((0, 8 - HEADS), (0, 0)))
    delta_top = lax.reduce_precision(delta, 8, 7)
    answers = jnp.concatenate([grad_att, delta_top.astype(BF16), (delta - delta_top).astype(BF16)], 0)
    do_halo = halo(mv, answers, False)

    dq, near, far = attend_queries(
        off, span, lohi, vec, q, grad_att, lse, delta, own_row, seg_col, kv_halo
    )
    out_recv = mv.rotate(after(out_other.astype(BF16), do_halo[0]), "c")
    outputs = (mixed + out_own + out_recv.astype(F32)).astype(BF16)
    swaps = [u.swap(do_halo[0]) for u in sums[0]]
    k_then = after(k, dq, *swaps)
    dk, dv = attend_keys(off, span, lohi, vec, k_then, v, seg_row, own_col, q_halo, do_halo)
    if small:
        dk = after(dk, *[u.inwards() for u in sums[0]])

    sheared = jnp.roll(jnp.sum(near, axis=1), BLK, axis=1)
    grad_table = jnp.dot(sheared, chosen.astype(F32), precision=lax.Precision.HIGHEST).T
    far_sums = jnp.sum(far, axis=(2, 3))
    grad_table = grad_table.at[31].add(far_sums[:, 0]).at[15].add(far_sums[:, 1])

    split = lambda x: x.reshape(n_seq, sc, rows)
    rows_z = jnp.concatenate([split(dq), split(dk), split(dv)], axis=1)
    grad_normed = jnp.einsum(
        "zdc,zct->dt", full[:, :, : 3 * sc], rows_z, preferred_element_type=F32
    )
    grad_source, grad_gain_one = norm_back(grad_normed, source, scale_one, gain_one)
    input_grad = (grad_mixed + grad_source).astype(BF16)

    gain_rows = jnp.concatenate(
        [grad_gain_one.reshape(n_dp, rw), grad_gain_two.reshape(n_dp, rw)], axis=1
    )
    widen = lambda x: jnp.pad(x, ((0, 0), (0, wide_cols - x.shape[1])))[:, None, :]
    extra = jnp.concatenate(
        [
            widen(gain_rows),
            widen(grad_table.reshape(n_dp, -1)),
            jnp.zeros((n_dp, rp - rw - 2, wide_cols), F32),
        ],
        axis=1,
    )
    core = mv.index["c"]
    if small and rw % 8 == 0 and rp % 16 == 0:
        send, keep = project(
            core.reshape(1).astype(jnp.int32), normed, grad_branch, dq, dk, dv, attended, extra, n_seq
        )
    else:
        g_in = jnp.einsum("dt,zct->zdc", normed, rows_z, preferred_element_type=F32)
        g_out = jnp.einsum("dt,zct->zdc", grad_branch, split(attended), preferred_element_type=F32)
        grads = jnp.concatenate([g_in, g_out], axis=2).reshape(n_seq, n_dp, rw, wide_cols)
        below = jnp.broadcast_to(extra[None], (n_seq,) + extra.shape)
        grads = jnp.concatenate([grads, below], axis=2).astype(BF16)
        grads = grads.reshape(n_seq, n_dp // 2, 2, rp, wide_cols)
        take = lambda c: jnp.moveaxis(lax.dynamic_index_in_dim(grads, c, 2, keepdims=False), 1, 0)
        send, keep = take(1 - core), take(core)
    if small:
        (first,), (wide, thin) = sums
        send = after(send, first.across())
        wide.swap(send)
    else:
        for units in sums[1:]:
            for u in units:
                u.swap(None)

    own, both = scatter_small(mv, send, keep)
    if small:
        thin.swap(both)
        first.home()
        for step in (ZSum.inwards, ZSum.across, ZSum.home):
            step(wide)
            step(thin)
    own_ffn = z_totals(mv, sums)

    return (
        outputs.T.reshape(seqs, rows, depth),
        input_grad.T.reshape(seqs, rows, depth),
        own[:rw, :sc],
        own[:rw, sc : 2 * sc],
        own[:rw, 2 * sc : 3 * sc],
        own[:rw, 3 * sc :].T,
        own_ffn[0],
        own_ffn[1],
        own_ffn[2].T,
        own[rw, :rw],
        own[rw, rw : 2 * rw],
        own[rw + 1, : table_row.shape[0]].reshape(rel_table.shape),
    )


def solution(mesh):
    row, col = P("dp", "seq"), P("seq", "dp")
    tokens = P("dp", "seq", None)
    return jax.shard_map(
        partial(on_device, mesh.shape["dp"], mesh.shape["seq"]),
        mesh=mesh,
        in_specs=(tokens, row, tokens, row, row, row, col, row, row, col, P("dp"), P("dp"), P("dp", None)),
        out_specs=(tokens, tokens, row, row, row, col, row, row, col, P("dp"), P("dp"), P("dp", None)),
        check_vma=False,
    )
```

```python
import math
from functools import partial

import jax
import jax.numpy as jnp
import numpy as np
from jax import lax
from jax.experimental import pallas as pl
from jax.experimental.pallas import tpu as pltpu
from jax.sharding import PartitionSpec as P

HEADS = 6
BUCKETS = 32
MAX_DOC = 800
BLK = 256
SPAN = 1024
EPS = 1e-06
MASKED = -1e30
F32 = jnp.float32
BF16 = jnp.bfloat16
VMEM_CAP = 58 * 1024 * 1024
LANES = 128
GELU_K = math.sqrt(2.0 / math.pi)
GELU_A = 0.044715


def bucket_table():
    relative = np.arange(SPAN) - SPAN // 2
    distance = np.abs(relative)
    steps = np.array([12, 16, 23, 32, 46, 64, 91])
    levels = (distance[:, None] >= steps[None, :]).sum(axis=1)
    inside = np.where(distance < 8, distance, 8 + levels)
    return (inside + 16 * (relative > 0)).astype(np.int32)


class Moves:
    def __init__(self, n_dp, n_seq):
        self.n_dp, self.n_seq = n_dp, n_seq
        plane = n_dp // 2
        side = int(round(math.sqrt(plane)))
        self.size = {"a": plane // side, "b": side, "c": 2, "z": n_seq}
        dp = lax.axis_index("dp")
        self.last = {}
        self.index = {
            "a": dp // (2 * side),
            "b": (dp // 2) % side,
            "c": dp % 2,
            "z": lax.axis_index("seq"),
        }

    def rotate(self, x, axis):
        n = self.size[axis]
        if axis == "z":
            return lax.ppermute(x, "seq", [(i, (i + 1) % n) for i in range(n)])
        pairs = []
        side = self.size["b"]
        for i in range(self.n_dp):
            a, b, c = i // (2 * side), (i // 2) % side, i % 2
            if axis == "a":
                a = (a + 1) % n
            elif axis == "b":
                b = (b + 1) % n
            else:
                c = 1 - c
            pairs.append((i, (a * side + b) * 2 + c))
        return lax.ppermute(x, "dp", pairs)

    def zperm(self, x, pairs):
        return lax.ppermute(x, "seq", pairs)

    def same_core(self):
        return [list(range(c, self.n_dp, 2)) for c in range(2)]

    def ring(self, x, waits=()):
        parts = []
        for step in range(self.n_seq - 1):
            x = self.rotate(after(x, *waits[step]) if step < len(waits) else x, "z")
            parts.append(x)
        return parts

    def gather(self, x, axis, at=0):
        n, i = self.size[axis], self.index[axis]
        if n == 2:
            other = self.rotate(x, axis)
            return ordered(i == 0, x, other, at)
        parts = [x]
        for _ in range(n - 1):
            parts.append(self.rotate(parts[-1], axis))
        turned = jnp.stack(parts[::-1] + parts[::-1], 0)
        full = lax.dynamic_slice_in_dim(turned, n - 1 - i, n, 0)
        return jnp.moveaxis(full, 0, at)

    def scatter(self, x, axis, at=0, out=BF16):
        n, i = self.size[axis], self.index[axis]
        take = lambda k: lax.dynamic_index_in_dim(x, k, at, keepdims=False)
        if n == 2:
            other = self.rotate(take(1 - i), axis)
            return add(take(i), other, out)
        acc = take((i + n - 1) % n)
        for step in range(n - 1):
            got = self.rotate(acc, axis)
            last = step == n - 2
            acc = add(take((i + 2 * n - 2 - step) % n), got, out if last else BF16)
        return acc


def after(x, *others):
    others = [o for o in others if o is not None]
    return lax.optimization_barrier((x, *others))[0] if others else x


def add(x, y, out):
    return (x.astype(F32) + y.astype(F32)).astype(out)


def ordered(first, x, y, at):
    return jnp.stack([jnp.where(first, x, y), jnp.where(first, y, x)], at)


def z_gather(mv, w, waits=()):
    z, n = mv.index["z"], mv.n_seq
    blocks = [w] + mv.ring(w, waits)
    turned = jnp.stack(blocks[::-1] + blocks[::-1], 0)
    return lax.dynamic_slice_in_dim(turned, n - 1 - z, n, 0)


def small_plane(mv):
    return mv.size["a"] == 2 and mv.size["b"] == 2 and mv.n_seq == 4


def gather_core(mv, w, ready):
    k, rows, cols = w.shape
    c = mv.index["c"]
    full = lax.all_gather(w, "seq")
    zh = mv.n_seq // 2
    keep = lax.dynamic_slice_in_dim(full, c * zh, zh, 0)
    send = lax.dynamic_slice_in_dim(full, (1 - c) * zh, zh, 0)
    recv = mv.rotate(after(send, *ready), "c")
    block = ordered(c == 0, keep, recv, 2)
    return [block[j].reshape(k, 2 * rows, cols) for j in range(zh)]


def scatter_plane(mv, grad):
    quarter, k, rows, cols = grad.shape
    chips = mv.n_dp // 2
    x = grad
    if chips != quarter:
        x = jnp.moveaxis(grad, 1, 0).reshape(k, chips, quarter * rows // chips, cols)
        x = jnp.moveaxis(x, 0, 1)
    x = lax.psum_scatter(x, "dp", scatter_dimension=0, axis_index_groups=mv.same_core())
    x = x.reshape(k, 2, x.shape[1] // 2, cols)
    return x


def swap_cores(mv, x):
    c = mv.index["c"]
    take = lambda i: lax.dynamic_index_in_dim(x, i, 1, keepdims=False)
    return take(c), mv.rotate(take(1 - c), "c")


class ZSum:
    def __init__(self, mv, j, x):
        self.mv, self.j, self.x = mv, j, x

    def swap(self, wait):
        c = self.mv.index["c"]
        x = after(self.x, wait)
        take = lambda i: lax.dynamic_index_in_dim(x, i, 1, keepdims=False)
        mine, other = take(c), self.mv.rotate(take(1 - c), "c")
        here = (self.mv.index["z"] // 2) == c
        self.pair = mine, other
        self.near, self.far = jnp.where(here, mine, other), jnp.where(here, other, mine)
        return other

    def inwards(self, wait=None):
        got = self.mv.zperm(after(self.far, wait), [(0, 1), (3, 2)])
        self.far = add(self.far, got, BF16)
        return got

    def across(self, wait=None):
        got = self.mv.zperm(after(self.far, wait), [(1, 2), (2, 1)])
        self.near = add(self.near, got, BF16)
        return got

    def home(self, wait=None):
        j = self.j
        got = self.mv.zperm(after(self.near, wait), [(1 - j, j), (3 - j, 2 + j)])
        self.total = add(self.near, got, F32)
        return got


def z_totals(mv, sums):
    z, c = mv.index["z"], mv.index["c"]
    join = lambda parts: jnp.concatenate(parts, 0)
    if mv.n_seq == 4:
        first, second = (join([u.total for u in units]) for units in sums)
        return jnp.where(z % 2 == 0, first, second)
    full = jnp.stack(
        [ordered(c == 0, *(join([u.pair[i] for u in units]) for i in range(2)), 0) for units in sums], 1
    )
    return mv.scatter(full.reshape((mv.n_seq,) + full.shape[2:]), "z", 0, F32)


def gather_small(mv, w):
    full = z_gather(mv, w)
    half = mv.n_seq // 2
    lo_one = mv.gather(full[:half], "b", 1)
    hi_one = mv.gather(full[half:], "a", 1)
    lo = mv.gather(lo_one, "a", 1)
    hi = mv.gather(hi_one, "b", 2)
    both = jnp.concatenate([lo, hi], 0)
    both = mv.gather(both, "c", 3)
    return both.reshape((mv.n_seq, mv.n_dp) + w.shape), (full, (lo_one, hi_one), (lo, hi))


def scatter_small(mv, send, keep):
    both = add(keep, mv.rotate(send, "c"), BF16)
    x = lax.psum_scatter(both, "dp", scatter_dimension=0, axis_index_groups=mv.same_core())
    return lax.psum_scatter(x, "seq", scatter_dimension=0).astype(F32), both


def reach_of(rows, n_seq):
    need, parts = MAX_DOC - 1, []
    while need > 0 and len(parts) + 1 < n_seq:
        parts.append(min(rows, -(-need // LANES) * LANES))
        need -= rows
    return parts


def halo(mv, x, chained=True):
    rows, n = x.shape[1], mv.n_seq
    left, right = [], []
    own = x
    for hop, cols in enumerate(reach_of(rows, n)):
        step = hop + 1
        if chained and hop > 0:
            x = after(x, left[0], right[-1])
        left.insert(0, mv.zperm(x[:, rows - cols :], [(i, i + step) for i in range(n - step)]))
        right.append(mv.zperm(x[:, :cols], [(i + step, i) for i in range(n - step)]))
    return left + [own] + right


def dot(x, y, dims):
    return lax.dot_general(x, y, (dims, ((), ())), preferred_element_type=F32)


def nt(x, y):
    return dot(x, y, ((1,), (1,)))


def nn(x, y):
    return dot(x, y, ((1,), (0,)))


def tn(x, y):
    return dot(x, y, ((0,), (0,)))


def make_tiles(vec_ref, tiles):
    for h in range(HEADS):
        line = vec_ref[h : h + 1, :]
        wide = jnp.broadcast_to(line, (BLK, SPAN))
        rolled = pltpu.roll(wide, 0, 1, stride=1, stride_axis=0)
        tiles[h * 5] = jnp.broadcast_to(line[:, :1], (BLK, BLK))
        tiles[h * 5 + 4] = jnp.broadcast_to(line[:, SPAN - 1 :], (BLK, BLK))
        for d in (-1, 0, 1):
            at = SPAN // 2 + BLK * d
            tiles[h * 5 + 2 + d] = rolled[:, at : at + BLK]


def class_of(query_block, key_block):
    return jnp.clip(query_block - key_block, -2, 2) + 2


def lay_out(off, pieces, whole):
    middle = len(pieces) // 2
    at = off - sum(p.shape[1] for p in pieces[:middle])
    if at > 0:
        whole[:, :at] = jnp.zeros((whole.shape[0], at), whole.dtype)
    for p in pieces:
        whole[:, at : at + p.shape[1]] = p[...]
        at += p.shape[1]
    if at < whole.shape[1]:
        whole[:, at:] = jnp.zeros((whole.shape[0], whole.shape[1] - at), whole.dtype)


def block_at(k):
    return pl.ds(pl.multiple_of(k * BLK, BLK), BLK)


def forward_kernel(off, count, lohi, vec, q_ref, segq, segk, *rest):
    pieces = rest[:count]
    out, exact, lse, split, tiles, kv = rest[count:]
    i = pl.program_id(0)

    @pl.when(i == 0)
    def _():
        make_tiles(vec, tiles)
        lay_out(off, pieces, kv)

    own = off // BLK + i
    inner = HEADS * 64
    low, high = lohi[i, 0], lohi[i, 1]
    seg_row = segq[0]
    split[...] = jnp.zeros_like(split)
    lse[...] = jnp.zeros_like(lse)
    for pair in range(HEADS // 2):
        heads = (2 * pair, 2 * pair + 1)
        qs = [q_ref[h * 64 : h * 64 + 64, :] for h in heads]

        def body(kb, state):
            cols = block_at(kb)
            same = segk[cols, :] == seg_row
            kind = class_of(own, kb)
            new = []
            for e, h in enumerate(heads):
                peak, total, acc = state[e]
                s = tn(kv[h * 64 : h * 64 + 64, cols], qs[e]) + tiles[h * 5 + kind]
                s = jnp.where(same, s, MASKED)
                top = jnp.maximum(peak, jnp.max(s, axis=0, keepdims=True))
                fade = jnp.exp(peak - top)
                p = jnp.exp(s - top)
                total = total * fade + jnp.sum(p, axis=0, keepdims=True)
                acc = acc * fade + nn(kv[inner + h * 64 : inner + h * 64 + 64, cols], p.astype(BF16))
                new.append((top, total, acc))
            return tuple(new)

        start = (
            jnp.full((1, BLK), MASKED, F32),
            jnp.zeros((1, BLK), F32),
            jnp.zeros((64, BLK), F32),
        )
        state = lax.fori_loop(low, high, body, (start, start))
        for e, h in enumerate(heads):
            peak, total, acc = state[e]
            done = acc / total
            out[h * 64 : h * 64 + 64, :] = done.astype(BF16)
            exact[h * 64 : h * 64 + 64, :] = done
            log = peak + jnp.log(total)
            lse[h : h + 1, :] = log
            for part in range(3):
                piece = log.astype(BF16)
                split[part * 8 + h : part * 8 + h + 1, :] = piece
                log = log - piece.astype(F32)


def query_kernel(off, count, lohi, vec, q_ref, do_ref, lse, delta, segq, segk, *rest):
    pieces = rest[:count]
    dq, near, far, tiles, sums, kv = rest[count:]
    i = pl.program_id(0)

    @pl.when(i == 0)
    def _():
        make_tiles(vec, tiles)
        lay_out(off, pieces, kv)
        sums[...] = jnp.zeros_like(sums)

    own = off // BLK + i
    inner = HEADS * 64
    low, high = lohi[i, 0], lohi[i, 1]
    seg_row = segq[0]
    for pair in range(HEADS // 2):
        heads = (2 * pair, 2 * pair + 1)
        qs = [q_ref[h * 64 : h * 64 + 64, :] for h in heads]
        dos = [do_ref[h * 64 : h * 64 + 64, :] for h in heads]

        def body(kb, state):
            cols = block_at(kb)
            same = segk[cols, :] == seg_row
            kind = class_of(own, kb)
            new = []
            for e, h in enumerate(heads):
                keys = kv[h * 64 : h * 64 + 64, cols]
                s = tn(keys, qs[e]) + tiles[h * 5 + kind]
                s = jnp.where(same, s, MASKED)
                p = jnp.exp(s - lse[h : h + 1, :])
                dp = tn(kv[inner + h * 64 : inner + h * 64 + 64, cols], dos[e])
                ds = p * (dp - delta[h : h + 1, :])
                at = h * 5 + kind
                sums[at] = sums[at] + ds
                new.append(state[e] + nn(keys, ds.astype(BF16)))
            return tuple(new)

        start = jnp.zeros((64, BLK), F32)
        state = lax.fori_loop(low, high, body, (start, start))
        for e, h in enumerate(heads):
            dq[h * 64 : h * 64 + 64, :] = state[e].astype(BF16)

    @pl.when(i == pl.num_programs(0) - 1)
    def _():
        for h in range(HEADS):
            zero = jnp.zeros((BLK, BLK), F32)
            x = jnp.concatenate([sums[h * 5 + 1], sums[h * 5 + 2], sums[h * 5 + 3], zero], axis=1)
            n = BLK // 2
            while n >= 8:
                x = x[:n] + pltpu.roll(x[n:], SPAN - n, 1)
                n //= 2
            row = lax.broadcasted_iota(jnp.int32, x.shape, 0)
            for n in (4, 2, 1):
                x = jnp.where((row & n) != 0, pltpu.roll(x, SPAN - n, 1), x)
            near[h] = x
            far[h, 0] = jnp.sum(sums[h * 5].reshape(BLK // 8, 8, BLK), axis=0)
            far[h, 1] = jnp.sum(sums[h * 5 + 4].reshape(BLK // 8, 8, BLK), axis=0)


def key_kernel(off, count, lohi, vec, k_ref, v_ref, segq, segk, *rest):
    queries, answers = rest[:count], rest[count : 2 * count]
    dk, dv, tiles, qs, dos = rest[2 * count :]
    i = pl.program_id(0)

    @pl.when(i == 0)
    def _():
        make_tiles(vec, tiles)
        lay_out(off, queries, qs)
        lay_out(off, answers, dos)

    own = off // BLK + i
    inner = HEADS * 64
    low, high = lohi[i, 0], lohi[i, 1]
    seg_col = segk[...]
    for pair in range(HEADS // 2):
        heads = (2 * pair, 2 * pair + 1)
        ks = [k_ref[h * 64 : h * 64 + 64, :] for h in heads]
        vs = [v_ref[h * 64 : h * 64 + 64, :] for h in heads]

        def body(qb, state):
            cols = block_at(qb)
            same = seg_col == segq[qb]
            kind = class_of(qb, own)
            logs = qs[inner : inner + 8, cols].astype(F32)
            logs = logs + qs[inner + 8 : inner + 16, cols].astype(F32)
            logs = logs + qs[inner + 16 : inner + 24, cols].astype(F32)
            deltas = dos[inner : inner + 8, cols].astype(F32)
            deltas = deltas + dos[inner + 8 : inner + 16, cols].astype(F32)
            new = []
            for e, h in enumerate(heads):
                q, do = qs[h * 64 : h * 64 + 64, cols], dos[h * 64 : h * 64 + 64, cols]
                s = tn(ks[e], q) + tiles[h * 5 + kind]
                s = jnp.where(same, s, MASKED)
                p = jnp.exp(s - logs[h : h + 1, :])
                ds = p * (tn(vs[e], do) - deltas[h : h + 1, :])
                to_k, to_v = state[e]
                new.append((to_k + nt(q, ds.astype(BF16)), to_v + nt(do, p.astype(BF16))))
            return tuple(new)

        start = jnp.zeros((64, BLK), F32)
        state = lax.fori_loop(low, high, body, ((start, start), (start, start)))
        for e, h in enumerate(heads):
            dk[h * 64 : h * 64 + 64, :] = state[e][0].astype(BF16)
            dv[h * 64 : h * 64 + 64, :] = state[e][1].astype(BF16)


def whole_block(shape):
    return pl.BlockSpec(shape, lambda i: (0,) * len(shape))


def col_block(rows):
    return pl.BlockSpec((rows, BLK), lambda i: (0, i))


SMEM_SPEC = pl.BlockSpec(memory_space=pltpu.SMEM)
COL_SEGS = pl.BlockSpec((BLK, 1), lambda i: (i, 0))
ROW_SEGS = pl.BlockSpec((1, 1, BLK), lambda i: (i, 0, 0))
TILES = pltpu.VMEM((HEADS * 5, BLK, BLK), F32)
LIGHT = pl.CostEstimate(flops=1, bytes_accessed=1, transcendentals=0)
ATTEND_COST = pl.CostEstimate(flops=23 * 10**9, bytes_accessed=1, transcendentals=0)
FFN_COST = pl.CostEstimate(flops=48 * 10**9, bytes_accessed=1, transcendentals=0)


def params():
    return pltpu.CompilerParams(
        dimension_semantics=("arbitrary",), vmem_limit_bytes=VMEM_CAP
    )


def attend(off, span, lohi, vec, q, seg_row, seg_col, kv):
    inner, rows = q.shape
    return pl.pallas_call(
        partial(forward_kernel, off, len(kv)),
        grid=(rows // BLK,),
        in_specs=[SMEM_SPEC, whole_block(vec.shape), col_block(inner), ROW_SEGS, whole_block(seg_col.shape)]
        + [whole_block(p.shape) for p in kv],
        out_specs=[col_block(inner), col_block(inner), col_block(8), col_block(32)],
        out_shape=[
            jax.ShapeDtypeStruct((inner, rows), BF16),
            jax.ShapeDtypeStruct((inner, rows), F32),
            jax.ShapeDtypeStruct((8, rows), F32),
            jax.ShapeDtypeStruct((32, rows), BF16),
        ],
        scratch_shapes=[TILES, pltpu.VMEM((2 * inner, span), BF16)],
        cost_estimate=ATTEND_COST,
        name="attend",
        compiler_params=params(),
    )(lohi, vec, q, seg_row, seg_col, *kv)


def attend_queries(off, span, lohi, vec, q, do, lse, delta, seg_row, seg_col, kv):
    inner, rows = q.shape
    return pl.pallas_call(
        partial(query_kernel, off, len(kv)),
        grid=(rows // BLK,),
        in_specs=[
            SMEM_SPEC,
            whole_block(vec.shape),
            col_block(inner),
            col_block(inner),
            col_block(8),
            col_block(8),
            ROW_SEGS,
            whole_block(seg_col.shape),
        ]
        + [whole_block(p.shape) for p in kv],
        out_specs=[
            col_block(inner),
            whole_block((HEADS, 8, SPAN)),
            whole_block((HEADS, 2, 8, BLK)),
        ],
        out_shape=[
            jax.ShapeDtypeStruct((inner, rows), BF16),
            jax.ShapeDtypeStruct((HEADS, 8, SPAN), F32),
            jax.ShapeDtypeStruct((HEADS, 2, 8, BLK), F32),
        ],
        scratch_shapes=[TILES, TILES, pltpu.VMEM((2 * inner, span), BF16)],
        cost_estimate=ATTEND_COST,
        name="attend_queries",
        compiler_params=params(),
    )(lohi, vec, q, do, lse, delta, seg_row, seg_col, *kv)


def attend_keys(off, span, lohi, vec, k, v, seg_row, seg_col, queries, answers):
    inner, rows = k.shape
    both = list(queries) + list(answers)
    return pl.pallas_call(
        partial(key_kernel, off, len(queries)),
        grid=(rows // BLK,),
        in_specs=[
            SMEM_SPEC,
            whole_block(vec.shape),
            col_block(inner),
            col_block(inner),
            whole_block(seg_row.shape),
            COL_SEGS,
        ]
        + [whole_block(p.shape) for p in both],
        out_specs=[col_block(inner), col_block(inner)],
        out_shape=[jax.ShapeDtypeStruct((inner, rows), BF16)] * 2,
        scratch_shapes=[
            TILES,
            pltpu.VMEM((queries[0].shape[0], span), BF16),
            pltpu.VMEM((answers[0].shape[0], span), BF16),
        ],
        cost_estimate=ATTEND_COST,
        name="attend_keys",
        compiler_params=params(),
    )(lohi, vec, k, v, seg_row, seg_col, *both)


def ffn_kernel(count, groups, order, na, nb, ca, cb, *rest):
    pieces = rest[:count]
    outs, grads = rest[count : count + 4], rest[count + 4 : count + 4 + len(groups)]
    weights, x, ct, hid, ggr, gur, sem = rest[count + 4 + len(groups) :]
    i = pl.program_id(0)
    t = na.shape[1]

    @pl.when(i == 0)
    def _():
        copies = []
        for piece in pieces:
            rows = piece.shape[2]
            for n in range(piece.shape[0]):
                k = len(copies) // 3
                at = pl.multiple_of(order[k], 16)
                for m in range(3):
                    copies.append(
                        pltpu.make_async_copy(
                            piece.at[n, m], weights.at[m, pl.ds(at, rows), :], sem.at[k, m]
                        )
                    )
        for copy in copies:
            copy.start()
        x[...] = na[...].T
        ct[...] = ca[...].T
        for copy in copies:
            copy.wait()

    @pl.when(i == 1)
    def _():
        x[...] = nb[...].T
        ct[...] = cb[...].T

    @pl.when(i < 2)
    def _():
        rows = pl.ds(pl.multiple_of(i * t, t), t)
        g = nn(x[...], weights[0])
        square = g * g
        th = jnp.tanh(GELU_K * g * (1.0 + GELU_A * square))
        part = 0.5 * (1.0 + th)
        gelu = g * part
        slope = part + 0.5 * g * (1.0 - th * th) * (GELU_K * (1.0 + 3.0 * GELU_A * square))
        u = nn(x[...], weights[1])
        h = (gelu * u).astype(BF16)
        gh = nn(ct[...], weights[2])
        gg = (gh * u * slope).astype(BF16)
        gu = (gh * gelu).astype(BF16)
        hid[rows, :] = h
        ggr[rows, :] = gg
        gur[rows, :] = gu
        out = nt(weights[2], h).astype(BF16)
        gn = (nt(weights[0], gg) + nt(weights[1], gu)).astype(BF16)

        @pl.when(i == 0)
        def _():
            outs[0][...] = out
            outs[2][...] = gn

        @pl.when(i == 1)
        def _():
            outs[1][...] = out
            outs[3][...] = gn

    @pl.when(i >= 2)
    def _():
        blocks, tile = grads[0].shape[0], grads[0].shape[2]
        size = blocks * tile
        rows = pl.ds(pl.multiple_of((i - 2) * size, 16), size)

        def product(first, second, right):
            return (nn(first[rows, :], right[:t, :]) + nn(second[rows, :], right[t:, :])).astype(BF16)

        lefts = ((na, nb, ggr), (na, nb, gur), (ca, cb, hid))
        for g, members in enumerate(groups):
            for n, m in enumerate(members):
                value = product(*lefts[m])
                for b in range(blocks):
                    grads[g][b, n] = value[b * tile : (b + 1) * tile]


def ffn(n_own, n_other, c_own, c_other, pieces, starts, groups):
    depth, t = n_own.shape
    cols = pieces[0].shape[3]
    tile = depth // 4
    scalars = jnp.stack([jnp.asarray(v, jnp.int32) for v in starts])
    whole = pl.BlockSpec((depth, t), lambda i, o: (0, 0), pipeline_mode=pl.Buffered(1))
    result = pl.BlockSpec((depth, t), lambda i, o: (0, 0))
    place = pl.BlockSpec(memory_space=pl.ANY)
    grads = [
        pl.BlockSpec((2, len(m), tile, cols), lambda i, o: (jnp.maximum(i - 2, 0), 0, 0, 0)) for m in groups
    ]
    return pl.pallas_call(
        partial(ffn_kernel, len(pieces), groups),
        grid_spec=pltpu.PrefetchScalarGridSpec(
            num_scalar_prefetch=1,
            grid=(4,),
            in_specs=[whole] * 4 + [place] * len(pieces),
            out_specs=[result] * 4 + grads,
            scratch_shapes=[
                pltpu.VMEM((3, depth, cols), BF16),
                pltpu.VMEM((t, depth), BF16),
                pltpu.VMEM((t, depth), BF16),
                pltpu.VMEM((2 * t, cols), BF16),
                pltpu.VMEM((2 * t, cols), BF16),
                pltpu.VMEM((2 * t, cols), BF16),
                pltpu.SemaphoreType.DMA((len(starts), 3)),
            ],
        ),
        out_shape=[jax.ShapeDtypeStruct((depth, t), BF16)] * 4
        + [jax.ShapeDtypeStruct((4, len(m), tile, cols), BF16) for m in groups],
        cost_estimate=FFN_COST,
        name="ffn",
        compiler_params=params(),
    )(scalars, n_own, n_other, c_own, c_other, *pieces)


def projection_kernel(rows, core, normed, branch, dq, dk, dv, att, extra, send, keep, left, right, value):
    t, cols = normed.shape[1], dq.shape[0]

    @pl.when(pl.program_id(0) == 0)
    def _():
        left[:, :t] = normed[...]
        left[:, t:] = branch[...]
        right[...] = jnp.zeros_like(right)

    for n, part in enumerate((dq, dk, dv)):
        right[n * cols : (n + 1) * cols, :t] = part[...]
    right[3 * cols :, t:] = att[...]
    value[...] = nt(left[...], right[...])
    for p in range(send.shape[0]):
        for ref, c in ((keep, core[0]), (send, 1 - core[0])):
            r = 2 * p + c
            block = value[pl.ds(pl.multiple_of(r * rows, 8), rows), :]
            ref[p, 0] = jnp.concatenate([block, extra[r]], axis=0).astype(BF16)


def project(core, normed, branch, dq, dk, dv, att, extra, n_seq):
    depth, t = normed.shape
    cols = dq.shape[0] // n_seq
    n_dp, more, wide = extra.shape
    rows = depth // n_dp
    whole = pl.BlockSpec((depth, t), lambda z: (0, 0))
    part = pl.BlockSpec((cols, t), lambda z: (z, 0))
    shape = (n_dp // 2, n_seq, rows + more, wide)
    result = pl.BlockSpec((n_dp // 2, 1) + shape[2:], lambda z: (0, z, 0, 0))
    return pl.pallas_call(
        partial(projection_kernel, rows),
        grid=(n_seq,),
        in_specs=[
            SMEM_SPEC,
            whole,
            whole,
            part,
            part,
            part,
            part,
            pl.BlockSpec(extra.shape, lambda z: (0, 0, 0)),
        ],
        out_specs=[result, result],
        out_shape=[jax.ShapeDtypeStruct(shape, BF16)] * 2,
        scratch_shapes=[
            pltpu.VMEM((depth, 2 * t), BF16),
            pltpu.VMEM((wide, 2 * t), BF16),
            pltpu.VMEM((depth, wide), F32),
        ],
        cost_estimate=pl.CostEstimate(flops=10**10, bytes_accessed=1, transcendentals=0),
        name="project",
        compiler_params=params(),
    )(core, normed, branch, dq, dk, dv, att, extra)


def rms_scale(x):
    return lax.rsqrt(jnp.mean(x * x, axis=0, keepdims=True) + EPS)


def norm_back(grad, x, scale, gain):
    gain_grad = jnp.sum(grad * (x * scale), axis=1)
    weighted = grad * gain
    dots = jnp.mean(weighted * x, axis=0, keepdims=True)
    return scale * weighted - x * (scale * scale * scale * dots), gain_grad


def on_device(
    n_dp,
    n_seq,
    inputs,
    segments,
    cotangent,
    w_query,
    w_key,
    w_value,
    w_out,
    w_gate,
    w_up,
    w_down,
    gain_attn,
    gain_ffn,
    rel_table,
):
    mv = Moves(n_dp, n_seq)
    seqs, rows, depth = inputs.shape
    source = inputs.reshape(seqs * rows, depth).T.astype(F32)
    tangent = cotangent.reshape(seqs * rows, depth).T
    rw, sc = w_query.shape
    inner = sc * n_seq
    wide_cols = 4 * sc
    seg_rows = -(-rows // wide_cols)
    rp = -(-(rw + 2 + seg_rows) // 16) * 16

    body = jnp.concatenate([w_query, w_key, w_value, w_out.T], axis=1)
    table_row = rel_table.reshape(-1)
    pad_to = lambda v: jnp.pad(v, (0, -v.shape[0] % wide_cols)).reshape(-1, wide_cols)
    packed = jnp.concatenate(
        [
            body,
            pad_to(jnp.concatenate([gain_attn, gain_ffn])),
            pad_to(table_row),
            pad_to(segments.reshape(rows).astype(BF16)),
            jnp.zeros((rp - rw - 2 - seg_rows, wide_cols), BF16),
        ],
        axis=0,
    )
    att, stages = gather_small(mv, packed)
    full = att[:, :, :rw, :].reshape(n_seq, depth, wide_cols)
    gain_one = att[0, :, rw, :rw].reshape(depth, 1).astype(F32)
    gain_two = att[0, :, rw, rw : 2 * rw].reshape(depth, 1).astype(F32)
    table = att[0, :, rw + 1, : table_row.shape[0]].reshape(BUCKETS, HEADS)
    here = lax.dynamic_index_in_dim(att, lax.axis_index("dp"), 1, keepdims=False)
    seg_seq = here[:, rw + 2 : rw + 2 + seg_rows, :].reshape(n_seq, -1)[:, :rows].astype(jnp.int32)

    scale_one = rms_scale(source)
    normed = ((source * scale_one) * gain_one).astype(BF16)
    qkv = jnp.einsum("zdc,dt->zct", full[:, :, : 3 * sc], normed, preferred_element_type=F32)
    qkv = jnp.transpose(qkv.astype(BF16).reshape(n_seq, 3, sc, rows), (1, 0, 2, 3))
    q = qkv[0].reshape(inner, rows)
    k = qkv[1].reshape(inner, rows)
    v = qkv[2].reshape(inner, rows)

    zh = n_seq // 2
    small = small_plane(mv)
    tangent_other = mv.rotate(tangent, "c")
    cores = gather_core(mv, jnp.stack([w_gate, w_up, w_down.T]), (q, tangent_other))
    kv_halo = halo(mv, after(jnp.concatenate([k, v], 0), cores[0]))
    pieces, starts = [], []
    for j in range(zh):
        full_block = lax.all_gather(cores[j], "dp", axis_index_groups=mv.same_core())
        if small:
            pieces.append([full_block])
            starts.append([jnp.int32(2 * rw * k) for k in range(4)])
        else:
            pieces.append([jnp.moveaxis(full_block, 0, 1).reshape(1, 3, depth, -1)])
            starts.append([jnp.int32(0)])

    off = -(-MAX_DOC // BLK) * BLK
    span = 2 * off + rows
    blocks = span // BLK
    seg_own = segments.reshape(rows)
    line = jnp.pad(seg_seq.reshape(-1), (off, off), constant_values=-1)
    seg_all = lax.dynamic_slice_in_dim(line, mv.index["z"] * rows, span, 0)
    seg_row = seg_all.reshape(blocks, 1, BLK)
    seg_col = seg_all.reshape(span, 1)
    own_row = seg_own.reshape(rows // BLK, 1, BLK)
    own_col = seg_own.reshape(rows, 1)
    spots = jnp.arange(span, dtype=jnp.int32)
    firsts = seg_own[::BLK]
    lasts = seg_own[BLK - 1 :: BLK]
    low = jnp.min(jnp.where(seg_all[None] == firsts[:, None], spots[None], 1 << 20), axis=1) // BLK
    high = jnp.max(jnp.where(seg_all[None] == lasts[:, None], spots[None], -1), axis=1) // BLK + 1
    lohi = jnp.stack([low, high], 1).astype(jnp.int32)

    buckets = bucket_table()
    buckets = np.concatenate([buckets[-1:], buckets[:0:-1]])
    chosen = jnp.asarray((buckets[:, None] == np.arange(BUCKETS)[None, :]), BF16)
    vec = dot(table, chosen, ((0,), (1,)))

    attended, exact, lse, lse_parts = attend(
        off, span, lohi, vec, q, own_row, seg_col, kv_halo
    )
    q_halo = halo(mv, jnp.concatenate([q, lse_parts], 0))

    mixed = source + jnp.einsum(
        "zdc,zct->dt", full[:, :, 3 * sc :], attended.reshape(n_seq, sc, rows), preferred_element_type=F32
    )
    scale_two = rms_scale(mixed)
    normed_two = ((mixed * scale_two) * gain_two).astype(BF16)

    normed_other = mv.rotate(normed_two, "c")
    parts, sums = [], []
    for j in range(zh):
        results = ffn(
            after(normed_two, *(list(parts[-1]) + q_halo if j else ())),
            normed_other,
            tangent,
            tangent_other,
            pieces[j],
            starts[j],
            ((0, 1, 2),) if j + 1 < zh else ((0, 1), (2,)),
        )
        parts.append(results[:4])
        sums.append([ZSum(mv, j, scatter_plane(mv, grad)) for grad in results[4:]])
    out_own, out_other, gn_own, gn_other = (
        sum(four[m].astype(F32) for four in parts) for m in range(4)
    )
    gn_recv = mv.rotate(gn_other.astype(BF16), "c")
    grad_n2 = gn_own + gn_recv.astype(F32)

    grad_mixed, grad_gain_two = norm_back(grad_n2, mixed, scale_two, gain_two)
    grad_mixed = grad_mixed + tangent.astype(F32)
    grad_branch = grad_mixed.astype(BF16)
    grad_att = jnp.einsum(
        "zdc,dt->zct", full[:, :, 3 * sc :], grad_branch, preferred_element_type=F32
    )
    grad_att = grad_att.reshape(inner, rows).astype(BF16)
    delta = jnp.sum((grad_att.astype(F32) * exact).reshape(HEADS, inner // HEADS, rows), axis=1)
    delta = jnp.pad(delta, ((0, 8 - HEADS), (0, 0)))
    delta_top = lax.reduce_precision(delta, 8, 7)
    answers = jnp.concatenate([grad_att, delta_top.astype(BF16), (delta - delta_top).astype(BF16)], 0)
    do_halo = halo(mv, answers, False)

    dq, near, far = attend_queries(
        off, span, lohi, vec, q, grad_att, lse, delta, own_row, seg_col, kv_halo
    )
    out_recv = mv.rotate(after(out_other.astype(BF16), do_halo[0]), "c")
    outputs = (mixed + out_own + out_recv.astype(F32)).astype(BF16)
    swaps = [u.swap(do_halo[0]) for u in sums[0]]
    k_then = after(k, dq)
    dk, dv = attend_keys(off, span, lohi, vec, k_then, v, seg_row, own_col, q_halo, do_halo)
    if small:
        dk = after(dk, *swaps)

    sheared = jnp.roll(jnp.sum(near, axis=1), BLK, axis=1)
    grad_table = jnp.dot(sheared, chosen.astype(F32), precision=lax.Precision.HIGHEST).T
    far_sums = jnp.sum(far, axis=(2, 3))
    grad_table = grad_table.at[31].add(far_sums[:, 0]).at[15].add(far_sums[:, 1])

    split = lambda x: x.reshape(n_seq, sc, rows)
    rows_z = jnp.concatenate([split(dq), split(dk), split(dv)], axis=1)
    grad_normed = jnp.einsum(
        "zdc,zct->dt", full[:, :, : 3 * sc], rows_z, preferred_element_type=F32
    )
    grad_source, grad_gain_one = norm_back(grad_normed, source, scale_one, gain_one)
    input_grad = (grad_mixed + grad_source).astype(BF16)

    gain_rows = jnp.concatenate(
        [grad_gain_one.reshape(n_dp, rw), grad_gain_two.reshape(n_dp, rw)], axis=1
    )
    widen = lambda x: jnp.pad(x, ((0, 0), (0, wide_cols - x.shape[1])))[:, None, :]
    extra = jnp.concatenate(
        [
            widen(gain_rows),
            widen(grad_table.reshape(n_dp, -1)),
            jnp.zeros((n_dp, rp - rw - 2, wide_cols), F32),
        ],
        axis=1,
    )
    core = mv.index["c"]
    if small and rw % 8 == 0 and rp % 16 == 0:
        send, keep = project(
            core.reshape(1).astype(jnp.int32), normed, grad_branch, dq, dk, dv, attended, extra, n_seq
        )
    else:
        g_in = jnp.einsum("dt,zct->zdc", normed, rows_z, preferred_element_type=F32)
        g_out = jnp.einsum("dt,zct->zdc", grad_branch, split(attended), preferred_element_type=F32)
        grads = jnp.concatenate([g_in, g_out], axis=2).reshape(n_seq, n_dp, rw, wide_cols)
        below = jnp.broadcast_to(extra[None], (n_seq,) + extra.shape)
        grads = jnp.concatenate([grads, below], axis=2).astype(BF16)
        grads = grads.reshape(n_seq, n_dp // 2, 2, rp, wide_cols)
        take = lambda c: jnp.moveaxis(lax.dynamic_index_in_dim(grads, c, 2, keepdims=False), 1, 0)
        send, keep = take(1 - core), take(core)
    if small:
        (first,), (wide, thin) = sums
        send = after(send, first.inwards())
        wide.swap(send)
    else:
        for units in sums[1:]:
            for u in units:
                u.swap(None)

    own, both = scatter_small(mv, send, keep)
    if small:
        thin.swap(both)
        first.across()
        first.home()
        for step in (ZSum.inwards, ZSum.across, ZSum.home):
            step(wide)
            step(thin)
    own_ffn = z_totals(mv, sums)

    return (
        outputs.T.reshape(seqs, rows, depth),
        input_grad.T.reshape(seqs, rows, depth),
        own[:rw, :sc],
        own[:rw, sc : 2 * sc],
        own[:rw, 2 * sc : 3 * sc],
        own[:rw, 3 * sc :].T,
        own_ffn[0],
        own_ffn[1],
        own_ffn[2].T,
        own[rw, :rw],
        own[rw, rw : 2 * rw],
        own[rw + 1, : table_row.shape[0]].reshape(rel_table.shape),
    )


def solution(mesh):
    row, col = P("dp", "seq"), P("seq", "dp")
    tokens = P("dp", "seq", None)
    return jax.shard_map(
        partial(on_device, mesh.shape["dp"], mesh.shape["seq"]),
        mesh=mesh,
        in_specs=(tokens, row, tokens, row, row, row, col, row, row, col, P("dp"), P("dp"), P("dp", None)),
        out_specs=(tokens, tokens, row, row, row, col, row, row, col, P("dp"), P("dp"), P("dp", None)),
        check_vma=False,
    )
```
